1024 devices in a mesh: dp: 64 (over x, y, core), mp: 16 (over z).
Axes of the slice: x: 4, y: 8, z: 16, core: 2. Of those that a mesh axis runs over, the one named last changes fastest.
Arguments:
- statistics: bfloat16 [128, 8192, 512], P('dp', 'mp'), as said below
- gradients: bfloat16 [128, 16, 512, 512], P('dp', None, 'mp'), may hold values from -6 to 6
- counts: int32 [64], P('dp'), may hold values from 0 to 2, as said below
Outputs:
- preconditioned: bfloat16 [128, 16, 512, 512], P('dp', None, 'mp')
The draws below stay inside these ranges and needn't reach their ends.
Inputs may be any that keep to these rules, and one draw needn't show every extreme that they name: counts[2 i] + counts[2 i + 1] == 2 for every i < 32, and some owner has 2. `statistics`: each statistic block is symmetric positive definite.
All inputs are finite; a program needn't handle non-finite values.
Results may differ from the reference program's by a relative error of at most 0.0067.
Values may be sent and summed in bfloat16 or wider, within the bound.
A program may use at most 32 MiB of HBM per device.

```python
import math
import jax
import jax.numpy as jnp
from jax import lax

B = 512
CAP = 2
SLOTS = 128
N_DP = 64
N_MP = 16


def draw_statistics(key, part):
    key = jax.random.fold_in(key, 11)
    identity = jnp.eye(B, dtype=jnp.float32)

    def one_block(index):
        block_key = jax.random.fold_in(key, index)
        key_rows, key_cols, key_factor = jax.random.split(block_key, 3)
        row_scale = jnp.exp(jax.random.uniform(key_rows, (B,), jnp.float32, 0.0, 0.5 * math.log(10.0)))
        col_scale = jnp.exp(jax.random.uniform(key_cols, (B,), jnp.float32, 0.0, math.log(10.0)))
        factor = jax.random.normal(key_factor, (B, B), jnp.float32)
        weighted = factor * col_scale[None, :]
        gram = jnp.dot(weighted, weighted.T, precision=lax.Precision.HIGHEST) / B
        gram = 0.5 * (gram + gram.T)
        matrix = row_scale[:, None] * row_scale[None, :] * (gram + 2.0 * identity)
        return matrix / (16.0 * math.sqrt(B))
    blocks = lax.map(one_block, jnp.arange(N_DP * CAP * N_MP, dtype=jnp.int32))
    return blocks.reshape(N_DP * CAP, N_MP * B, B).astype(jnp.bfloat16)


def draw_counts(key, part):
    key = jax.random.fold_in(key, 12)
    first_of_pair = jax.random.randint(key, (N_DP // 2,), 0, 3, jnp.int32)
    first_of_pair = first_of_pair.at[0].set(2)
    paired = jnp.stack([first_of_pair, 2 - first_of_pair], axis=1)
    return paired.reshape(N_DP).astype(jnp.int32)


def block_scale(rng, shape, cuts, least, top_value):
    def one(axis_at, blocks):
        steps = jax.random.uniform(jax.random.fold_in(jax.random.fold_in(rng, 6), axis_at), (blocks,), jnp.float32, least / len(cuts), top_value / len(cuts))
        return jnp.repeat(jnp.exp(steps), shape[axis_at] // blocks).reshape((-1,) + (1,) * (len(shape) - axis_at - 1))

    gain = one(*cuts[0])
    for cut in cuts[1:]:
        gain = gain * one(*cut)
    return gain


def scatter_about(key, dims, scale, limit, cuts=(), held_as=jnp.bfloat16):
    values = jax.random.normal(key, dims, jnp.float32) * scale
    if len(cuts) > 0:
        values = block_scale(key, dims, cuts, -0.22, 0.18) * values
    return jnp.clip(values, min=-limit, max=limit).astype(held_as)


def setup_inputs(seed: int = 0) -> dict:
    key_of = jax.random.split(jax.random.key(seed), 4)
    statistics = draw_statistics(jax.random.fold_in(key_of[3], 71), 0)
    gradients = scatter_about(key_of[1], (SLOTS, N_MP, B, B), 1.0, 6.0, ((0, 64), (2, 16)))
    counts = draw_counts(jax.random.fold_in(key_of[3], 71), 0)
    return dict(statistics=statistics, gradients=gradients, counts=counts)


def newton_root(block):
    values = block.astype(jnp.float32)
    norm_scale = jnp.sqrt(jnp.sum(values * values)) + 1e-06
    scaled = (values / norm_scale).astype(jnp.bfloat16)
    identity = jnp.eye(B, dtype=jnp.float32)
    step_one = ((5.0 * identity - scaled.astype(jnp.float32)) * 0.25).astype(jnp.bfloat16)
    square = jnp.dot(step_one, step_one, preferred_element_type=jnp.float32).astype(jnp.bfloat16)
    fourth = jnp.dot(square, square, preferred_element_type=jnp.float32).astype(jnp.bfloat16)
    updated = jnp.dot(fourth, scaled, preferred_element_type=jnp.float32)
    step_two = ((5.0 * identity - updated) * 0.25).astype(jnp.bfloat16)
    product = jnp.dot(step_one, step_two, preferred_element_type=jnp.float32)
    return (product * norm_scale ** (-0.25)).astype(jnp.bfloat16)

def reference(statistics, gradients, counts):

    def one_block(index):
        slot_row = (index // N_MP).astype(jnp.int32)
        block_index = (index % N_MP).astype(jnp.int32)
        owner = slot_row // CAP
        is_live = slot_row % CAP < counts[owner]

        def compute(unused):
            block = lax.dynamic_slice(statistics, (slot_row, block_index * B, jnp.int32(0)), (1, B, B))[0]
            grad_block = lax.dynamic_slice(gradients, (slot_row, block_index, jnp.int32(0), jnp.int32(0)), (1, 1, B, B))[0, 0]
            inv_root = newton_root(block)
            return jnp.dot(grad_block, inv_root.T, preferred_element_type=jnp.float32).astype(jnp.bfloat16)

        def empty(unused):
            return jnp.zeros((B, B), jnp.bfloat16)
        return lax.cond(is_live, compute, empty, 0)
    indices = jnp.arange(N_DP * CAP * N_MP, dtype=jnp.int32)
    result = lax.map(one_block, indices)
    return result.reshape(N_DP * CAP, N_MP, B, B)
```

```python
import functools
import jax
import jax.numpy as jnp
from jax import lax
from jax.sharding import PartitionSpec as P


def newton(blocks):
    order = blocks.shape[-1]
    values = blocks.astype(jnp.float32)
    norm_scale = jnp.sqrt(jnp.sum(values * values, axis=(1, 2))) + 1e-06
    scaled = (values / norm_scale[:, None, None]).astype(jnp.bfloat16)
    identity = jnp.eye(order, dtype=jnp.float32)
    step_one = ((5.0 * identity - scaled.astype(jnp.float32)) * 0.25).astype(jnp.bfloat16)
    square = jnp.einsum(
        "nij,njk->nik", step_one, step_one, preferred_element_type=jnp.float32
    ).astype(jnp.bfloat16)
    fourth = jnp.einsum("nij,njk->nik", square, square, preferred_element_type=jnp.float32).astype(
        jnp.bfloat16
    )
    updated = jnp.einsum("nij,njk->nik", fourth, scaled, preferred_element_type=jnp.float32)
    step_two = ((5.0 * identity - updated) * 0.25).astype(jnp.bfloat16)
    product = jnp.einsum("nij,njk->nik", step_one, step_two, preferred_element_type=jnp.float32)
    return (product * (norm_scale ** (-0.25))[:, None, None]).astype(jnp.bfloat16)


def sibling(mesh, value):
    size = mesh.shape["dp"]
    return lax.ppermute(value, "dp", [(at, at ^ 1) for at in range(size)])


def on_device(mesh, statistics, gradients, counts):
    count = counts[0]
    order = statistics.shape[2]
    own_first = count >= 1
    block = jnp.where(own_first, statistics[0], sibling(mesh, statistics[1]))
    rows = jnp.where(own_first, gradients[0], sibling(mesh, gradients[1]))
    columns = lax.all_to_all(rows, "mp", split_axis=0, concat_axis=1, tiled=True)
    inv_root = newton(block.reshape(1, order, order))[0]
    product = jnp.einsum(
        "kj,ij->ki", columns[0], inv_root, preferred_element_type=jnp.float32
    ).astype(jnp.bfloat16)
    result = lax.all_to_all(product[None], "mp", split_axis=1, concat_axis=0, tiled=True)
    other = sibling(mesh, result)
    zero = jnp.zeros_like(result)
    first = jnp.where(own_first, result, zero)
    second = jnp.where(count >= 2, other, zero)
    return jnp.stack([first, second])


def solution(mesh):
    in_specs = (P("dp", "mp", None), P("dp", None, "mp", None), P("dp"))
    out_specs = P("dp", None, "mp", None)
    return jax.shard_map(
        functools.partial(on_device, mesh),
        mesh=mesh,
        in_specs=in_specs,
        out_specs=out_specs,
        check_vma=False,
    )
```

```python
import functools

import jax
import jax.numpy as jnp
from jax import lax
from jax.experimental import pallas as pl
from jax.experimental.pallas import tpu as pltpu
from jax.sharding import PartitionSpec as P

MESH = pl.DeviceIdType.MESH
LANES = 128
TAIL = 16
F32 = jnp.float32
BF16 = jnp.bfloat16


def dot(a, b):
    return jnp.dot(a, b, preferred_element_type=F32)


def dot_t(a, b):
    return lax.dot_general(a, b, (((1,), (1,)), ((), ())), preferred_element_type=F32)


def iotas(shape):
    return lax.broadcasted_iota(jnp.int32, shape, 0), lax.broadcasted_iota(jnp.int32, shape, 1)


def newton_root(block):
    order = block.shape[0]
    values = block.astype(F32)
    total = jnp.sum(jnp.sum(values * values, axis=1, keepdims=True), axis=0, keepdims=True)
    norm_scale = jnp.sqrt(total) + 1e-06
    scaled = (values * (1.0 / norm_scale)).astype(BF16)
    row, column = iotas((order, order))
    five = jnp.where(row == column, 5.0, 0.0).astype(F32)
    step_one = ((five - scaled.astype(F32)) * 0.25).astype(BF16)
    square = dot(step_one, step_one).astype(BF16)
    fourth = dot(square, square).astype(BF16)
    updated = dot(fourth, scaled)
    step_two = ((five - updated) * 0.25).astype(BF16)
    return dot(step_one, step_two) * lax.rsqrt(jnp.sqrt(norm_scale))


def pack(root, ref):
    half = root.shape[0] // 2
    slabs = half // LANES
    row, column = iotas((half, half))
    corner = root[half:, half:]
    across = root[:half, half:].astype(BF16)
    both = jnp.where(row <= column, root[:half, :half], corner).astype(BF16)
    diagonal = jnp.sum(jnp.where(row == column, corner, 0.0), axis=0, keepdims=True)
    tail_row, _ = iotas((TAIL, LANES))
    tail = jnp.zeros((TAIL, LANES), F32)
    for j in range(slabs):
        lanes = slice(j * LANES, (j + 1) * LANES)
        ref[j * half : (j + 1) * half, :] = across[:, lanes]
        ref[(slabs + j) * half : (slabs + j + 1) * half, :] = both[:, lanes]
        tail = jnp.where(tail_row == j, diagonal[:, lanes], tail)
    ref[2 * slabs * half :, :] = tail.astype(BF16)


def unpack(ref, half):
    slabs = half // LANES
    row, column = iotas((half, half))
    across = jnp.concatenate([ref[j * half : (j + 1) * half, :] for j in range(slabs)], axis=1)
    both = jnp.concatenate(
        [ref[(slabs + j) * half : (slabs + j + 1) * half, :] for j in range(slabs)], axis=1
    ).astype(F32)
    tail = ref[2 * slabs * half :, :].astype(F32)
    diagonal = jnp.concatenate([tail[j : j + 1, :] for j in range(slabs)], axis=1)
    mirror = both.T
    first = jnp.where(row <= column, both, mirror).astype(BF16)
    last = jnp.where(row > column, both, jnp.where(row == column, diagonal, mirror)).astype(BF16)
    return first, across, last


def apply_root(rows, ref):
    half = rows.shape[1] // 2
    first, across, last = unpack(ref, half)
    left, right = rows[:, :half], rows[:, half:]
    out_left = dot(left, first) + dot_t(right, across)
    out_right = dot(left, across) + dot(right, last)
    return jnp.concatenate([out_left, out_right], axis=1).astype(BF16)


def kernel(
    ring,
    reach,
    counts_ref,
    stat_ref,
    grad_ref,
    out_ref,
    stat_own,
    stat_sib,
    grad_own,
    grad_sib,
    grad_sel,
    request,
    answer,
    own_root,
    roots,
    result,
    local_sem,
    sib_send,
    sib_recv,
    row_send,
    row_recv,
    root_send,
    root_recv,
    back_send,
    back_recv,
    out_local,
    out_send,
    out_recv,
):
    dp, me = lax.axis_index("dp"), lax.axis_index("mp")
    core = lax.rem(dp, 2)
    sibling = {"dp": dp + 1 - 2 * core}
    sign = 1 - 2 * core
    order = stat_own.shape[0]
    half = order // 2
    chunks = 2 * half // LANES
    height = grad_own.shape[1]

    def at(offset):
        return lax.rem(me + sign * offset + 4 * ring, ring)

    def to(offset):
        return {"mp": at(offset)}

    stat_copy = pltpu.make_async_copy(stat_ref.at[0], stat_own, local_sem.at[0])
    grad_copy = pltpu.make_async_copy(grad_ref.at[0], grad_own, local_sem.at[1])
    grad_copy.start()
    stat_copy.start()

    barrier = pltpu.get_barrier_semaphore()
    pl.semaphore_signal(barrier, inc=1, device_id=sibling, device_id_type=MESH)
    for d in range(1, reach + 1):
        pl.semaphore_signal(barrier, inc=1, device_id=to(d), device_id_type=MESH)
        pl.semaphore_signal(barrier, inc=1, device_id=to(-d), device_id_type=MESH)
    pl.semaphore_wait(barrier, 2 * reach + 1)

    def far_first(j):
        return lax.rem(me + reach + 1 + j, ring)

    def grad_swap(j):
        block = far_first(j)
        return pltpu.make_async_remote_copy(
            src_ref=grad_ref.at[1, block],
            dst_ref=grad_sib.at[block],
            send_sem=sib_send.at[j],
            recv_sem=sib_recv.at[j],
            device_id=sibling,
            device_id_type=MESH,
        )

    stat_swap = pltpu.make_async_remote_copy(
        src_ref=stat_ref.at[1],
        dst_ref=stat_sib,
        send_sem=sib_send.at[ring],
        recv_sem=sib_recv.at[ring],
        device_id=sibling,
        device_id_type=MESH,
    )
    far = ring - 2 * reach - 1
    for j in range(far):
        grad_swap(j).start()
    stat_swap.start()
    for j in range(far, ring):
        grad_swap(j).start()

    own_first = counts_ref[0] >= 1

    def select_rows(j):
        grad_swap(j).wait_recv()
        block = far_first(j)
        grad_sel[block] = jnp.where(own_first, grad_own[block], grad_sib[block])

    grad_copy.wait()
    far_sides = [(1, k) for k in range(1, ring // 2 - reach + 1)]
    far_sides += [(0, k) for k in range(1, ring // 2 - reach)]

    def row_copy(side, k):
        way = 1 if side else -1
        return pltpu.make_async_remote_copy(
            src_ref=grad_sel.at[at(way * (reach + k))],
            dst_ref=request.at[side, pl.ds(k * height, height)],
            send_sem=row_send.at[side, k],
            recv_sem=row_recv.at[side, k],
            device_id=to(way * k),
            device_id_type=MESH,
        )

    for j in range(far):
        select_rows(j)
    for side, k in far_sides:
        row_copy(side, k).start()

    stat_copy.wait()
    stat_swap.wait_recv()
    pack(newton_root(jnp.where(own_first, stat_own[...], stat_sib[...])), own_root)

    def piece(c):
        return pl.ds(c * half, half if c < chunks - 1 else half + TAIL)

    def root_copy(side, d, c):
        source = own_root if d == 1 else roots.at[side, d - 2]
        return pltpu.make_async_remote_copy(
            src_ref=source.at[piece(c)],
            dst_ref=roots.at[side, d - 1, piece(c)],
            send_sem=root_send.at[side, d - 1, c],
            recv_sem=root_recv.at[side, d - 1, c],
            device_id=to(-1 if side else 1),
            device_id_type=MESH,
        )

    for c in range(chunks):
        for side in range(2):
            root_copy(side, 1, c).start()

    for j in range(far, ring):
        select_rows(j)

    def out_copies(slot, block):
        local = pltpu.make_async_copy(result.at[block], out_ref.at[0, block], out_local.at[slot])
        remote = pltpu.make_async_remote_copy(
            src_ref=result.at[block],
            dst_ref=out_ref.at[1, block],
            send_sem=out_send.at[slot],
            recv_sem=out_recv.at[slot],
            device_id=sibling,
            device_id_type=MESH,
        )
        return local, remote

    def out_slot(offset):
        return lax.rem(sign * offset + 4 * ring, ring)

    def send_out(offset):
        for copy in out_copies(out_slot(offset), at(offset)):
            copy.start()

    result[me] = apply_root(grad_sel[me], own_root)
    send_out(0)

    for d in range(1, reach + 1):
        for c in range(chunks):
            for side in range(2):
                root_copy(side, d, c).wait_recv()
                if d < reach:
                    root_copy(side, d + 1, c).start()
        if d < reach:
            for side in range(2):
                offset = d if side else -d
                result[at(offset)] = apply_root(grad_sel[at(offset)], roots.at[side, d - 1])
                send_out(offset)

    def back_copy(side, k):
        way = 1 if side else -1
        return pltpu.make_async_remote_copy(
            src_ref=answer.at[side, pl.ds(k * height, height)],
            dst_ref=result.at[at(way * reach)],
            send_sem=back_send.at[side, k],
            recv_sem=back_recv.at[side, k],
            device_id=to(-way * k),
            device_id_type=MESH,
        )

    def arrived(side, k):
        way = 1 if side else -1
        return pltpu.make_async_remote_copy(
            src_ref=answer.at[side, pl.ds(k * height, height)],
            dst_ref=result.at[at(way * (reach + k))],
            send_sem=back_send.at[side, k],
            recv_sem=back_recv.at[side, k],
            device_id=to(way * k),
            device_id_type=MESH,
        )

    for side in (1, 0):
        way = 1 if side else -1
        served = [k for s, k in far_sides if s == side]
        for k in served:
            row_copy(side, k).wait_recv()
        request[side, 0:height] = grad_sel[at(way * reach)]
        tall = (len(served) + 1) * height
        answer[side, 0:tall] = apply_root(request[side, 0:tall], roots.at[side, reach - 1])
        for k in reversed(served):
            back_copy(side, k).start()
        result[at(way * reach)] = answer[side, 0:height]
        send_out(way * reach)

    for side, k in sorted(far_sides, key=lambda each: each[1]):
        arrived(side, k).wait_recv()
        send_out((1 if side else -1) * (reach + k))

    for j in range(ring):
        grad_swap(j).wait_send()
    stat_swap.wait_send()
    for side, k in far_sides:
        row_copy(side, k).wait_send()
        back_copy(side, k).wait_send()
    for d in range(1, reach + 1):
        for c in range(chunks):
            for side in range(2):
                root_copy(side, d, c).wait_send()
    for offset in range(ring):
        local, remote = out_copies(offset, lax.rem(me + offset, ring))
        local.wait()
        remote.wait()


def on_device(mesh, statistics, gradients, counts):
    ring = mesh.shape["mp"]
    reach = ring // 4
    slots, blocks, height, order = gradients.shape
    half = order // 2
    chunks = 2 * half // LANES
    packed = chunks * half + TAIL
    tall = (ring // 2 - reach + 1) * height
    anywhere = pl.BlockSpec(memory_space=pl.ANY)
    dma = pltpu.SemaphoreType.DMA
    out = pl.pallas_call(
        functools.partial(kernel, ring, reach),
        out_shape=jax.ShapeDtypeStruct(gradients.shape, BF16),
        in_specs=[pl.BlockSpec(memory_space=pltpu.SMEM), anywhere, anywhere],
        out_specs=anywhere,
        scratch_shapes=[
            pltpu.VMEM((order, order), BF16),
            pltpu.VMEM((order, order), BF16),
            pltpu.VMEM((blocks, height, order), BF16),
            pltpu.VMEM((blocks, height, order), BF16),
            pltpu.VMEM((blocks, height, order), BF16),
            pltpu.VMEM((2, tall, order), BF16),
            pltpu.VMEM((2, tall, order), BF16),
            pltpu.VMEM((packed, LANES), BF16),
            pltpu.VMEM((2, reach, packed, LANES), BF16),
            pltpu.VMEM((blocks, height, order), BF16),
            dma((2,)),
            dma((ring + 1,)),
            dma((ring + 1,)),
            dma((2, ring // 2)),
            dma((2, ring // 2)),
            dma((2, reach, chunks)),
            dma((2, reach, chunks)),
            dma((2, ring // 2)),
            dma((2, ring // 2)),
            dma((ring,)),
            dma((ring,)),
            dma((ring,)),
        ],
        compiler_params=pltpu.CompilerParams(
            collective_id=0, has_side_effects=True, vmem_limit_bytes=40 * 1024 * 1024
        ),
        name="hybrid",
    )(counts, statistics, gradients)
    live = (jnp.arange(slots) < counts[0])[:, None, None, None]
    return jnp.where(live, out, jnp.zeros_like(out))


def solution(mesh):
    in_specs = (P("dp", "mp", None), P("dp", None, "mp", None), P("dp"))
    out_specs = P("dp", None, "mp", None)
    return jax.shard_map(
        functools.partial(on_device, mesh),
        mesh=mesh,
        in_specs=in_specs,
        out_specs=out_specs,
        check_vma=False,
    )
```

```python
import functools

import jax
import jax.numpy as jnp
from jax import lax
from jax.experimental import pallas as pl
from jax.experimental.pallas import tpu as pltpu
from jax.sharding import PartitionSpec as P

MESH = pl.DeviceIdType.MESH
LANES = 128
TAIL = 16
REACH = 4
RELAY = True
F32 = jnp.float32
BF16 = jnp.bfloat16


def dot(a, b):
    return jnp.dot(a, b, preferred_element_type=F32)


def dot_t(a, b):
    return lax.dot_general(a, b, (((1,), (1,)), ((), ())), preferred_element_type=F32)


def iotas(shape):
    return lax.broadcasted_iota(jnp.int32, shape, 0), lax.broadcasted_iota(jnp.int32, shape, 1)


def newton_root(block):
    order = block.shape[0]
    values = block.astype(F32)
    total = jnp.sum(jnp.sum(values * values, axis=1, keepdims=True), axis=0, keepdims=True)
    norm_scale = jnp.sqrt(total) + 1e-06
    scaled = (values * (1.0 / norm_scale)).astype(BF16)
    row, column = iotas((order, order))
    five = jnp.where(row == column, 5.0, 0.0).astype(F32)
    step_one = ((five - scaled.astype(F32)) * 0.25).astype(BF16)
    square = dot(step_one, step_one).astype(BF16)
    fourth = dot(square, square).astype(BF16)
    updated = dot(fourth, scaled)
    step_two = ((five - updated) * 0.25).astype(BF16)
    return dot(step_one, step_two) * lax.rsqrt(jnp.sqrt(norm_scale))


def layout(half):
    across = half * half // LANES
    corner = across // 2
    first = corner + TAIL
    return across, corner, [(0, across // 2), (across // 2, across // 2), (across, first), (across + first, corner)]


def fold(block):
    size = block.shape[0] // 2
    row, column = iotas((size, size))
    corner = block[size:, size:]
    both = jnp.where(row <= column, block[:size, :size], corner)
    diagonal = jnp.sum(jnp.where(row == column, corner, 0.0), axis=0, keepdims=True)
    return block[:size, size:].astype(BF16), both.astype(BF16), diagonal


def unfold(above, both, diagonal):
    size = both.shape[0]
    row, column = iotas((size, size))
    both = both.astype(F32)
    mirror = both.T
    first = jnp.where(row <= column, both, mirror).astype(BF16)
    last = jnp.where(row > column, both, jnp.where(row == column, diagonal, mirror)).astype(BF16)
    below = above.astype(F32).T.astype(BF16)
    return jnp.concatenate(
        [jnp.concatenate([first, above], axis=1), jnp.concatenate([below, last], axis=1)], axis=0
    )


def store_slabs(ref, start, block):
    height, width = block.shape
    for j in range(width // LANES):
        ref[start + j * height : start + (j + 1) * height, :] = block[:, j * LANES : (j + 1) * LANES]
    return start + height * width // LANES


def load_slabs(ref, start, height, width):
    slabs = [ref[start + j * height : start + (j + 1) * height, :] for j in range(width // LANES)]
    return jnp.concatenate(slabs, axis=1) if len(slabs) > 1 else slabs[0]


def pack(root, ref):
    half = root.shape[0] // 2
    size = half // 2
    across, corner, _ = layout(half)
    store_slabs(ref, 0, root[:half, half:].astype(BF16))
    above_0, both_0, diagonal_0 = fold(root[:half, :half])
    above_1, both_1, diagonal_1 = fold(root[half:, half:])
    end = store_slabs(ref, store_slabs(ref, across, above_0), both_0)
    tail_row, _ = iotas((TAIL, size))
    tail = jnp.where(tail_row == 0, diagonal_0, jnp.where(tail_row == 1, diagonal_1, 0.0))
    ref[end : end + TAIL, :] = tail.astype(BF16)
    store_slabs(ref, store_slabs(ref, end + TAIL, above_1), both_1)


def unpack_across(ref, half):
    return load_slabs(ref, 0, half, half)


def unpack_corner(ref, half, which):
    across, corner, _ = layout(half)
    size = half // 2
    start = across + which * (corner + TAIL)
    above = load_slabs(ref, start, size, size)
    both = load_slabs(ref, start + corner // 2, size, size)
    tail = ref[across + corner : across + corner + TAIL, :].astype(F32)
    return unfold(above, both, tail[which : which + 1, :])


def left_half(rows, ref):
    half = rows.shape[1] // 2
    left, right = rows[:, :half], rows[:, half:]
    return (dot(left, unpack_corner(ref, half, 0)) + dot_t(right, unpack_across(ref, half))).astype(BF16)


def right_half(rows, ref):
    half = rows.shape[1] // 2
    left, right = rows[:, :half], rows[:, half:]
    return (dot(left, unpack_across(ref, half)) + dot(right, unpack_corner(ref, half, 1))).astype(BF16)


def apply_root(rows, ref):
    return jnp.concatenate([left_half(rows, ref), right_half(rows, ref)], axis=1)


def kernel(
    ring,
    reach,
    counts_ref,
    stat_ref,
    grad_ref,
    out_ref,
    stat_own,
    stat_sib,
    grad_own,
    grad_sib,
    grad_sel,
    request,
    answer,
    own_root,
    roots,
    result,
    local_sem,
    sib_send,
    sib_recv,
    row_send,
    row_recv,
    root_send,
    root_recv,
    back_send,
    back_recv,
    out_local,
    out_send,
    out_recv,
    ready,
):
    dp, me = lax.axis_index("dp"), lax.axis_index("mp")
    core = lax.rem(dp, 2)
    sibling = {"dp": dp + 1 - 2 * core}
    sign = 1 - 2 * core
    order = stat_own.shape[0]
    half = order // 2
    pieces = layout(half)[2]
    chunks = len(pieces)
    height = grad_own.shape[1]

    def at(offset):
        return lax.rem(me + sign * offset + 4 * ring, ring)

    def to(offset):
        return {"mp": at(offset)}

    stat_copy = pltpu.make_async_copy(stat_ref.at[0], stat_own, local_sem.at[0])
    grad_copy = pltpu.make_async_copy(grad_ref.at[0], grad_own, local_sem.at[1])
    grad_copy.start()
    stat_copy.start()

    barrier = pltpu.get_barrier_semaphore()
    pl.semaphore_signal(barrier, inc=1, device_id=sibling, device_id_type=MESH)
    span = max(1, ring // 2 - reach)
    direct = 1 if RELAY else span
    for d in range(1, direct + 1):
        pl.semaphore_signal(barrier, inc=1, device_id=to(d), device_id_type=MESH)
        pl.semaphore_signal(barrier, inc=1, device_id=to(-d), device_id_type=MESH)
    pl.semaphore_wait(barrier, 2 * direct + 1)

    def tell(d):
        if RELAY and d <= span:
            pl.semaphore_signal(ready.at[0, d], inc=1, device_id=to(1), device_id_type=MESH)
            pl.semaphore_signal(ready.at[1, d], inc=1, device_id=to(-1), device_id_type=MESH)

    def heard(d):
        if RELAY and 1 < d <= span:
            pl.semaphore_wait(ready.at[0, d], 1)
            pl.semaphore_wait(ready.at[1, d], 1)
            tell(d + 1)

    tell(2)

    def grad_swap(block):
        j = lax.rem(block - me + ring, ring)
        return pltpu.make_async_remote_copy(
            src_ref=grad_ref.at[1, block],
            dst_ref=grad_sib.at[block],
            send_sem=sib_send.at[j],
            recv_sem=sib_recv.at[j],
            device_id=sibling,
            device_id_type=MESH,
        )

    stat_swap = pltpu.make_async_remote_copy(
        src_ref=stat_ref.at[1],
        dst_ref=stat_sib,
        send_sem=sib_send.at[ring],
        recv_sem=sib_recv.at[ring],
        device_id=sibling,
        device_id_type=MESH,
    )
    far_sides = [(1, ring // 2 - reach)]
    for k in range(ring // 2 - reach - 1, 0, -1):
        far_sides += [(1, k), (0, k)]
    nearest_first = far_sides[::-1]
    row_order = nearest_first if RELAY else far_sides

    def far_block(side, k):
        return at((1 if side else -1) * (reach + k))

    for side, k in row_order:
        grad_swap(far_block(side, k)).start()
    stat_swap.start()
    for d in range(-reach, reach + 1):
        grad_swap(at(d)).start()

    own_first = counts_ref[0] >= 1

    def select_rows(block):
        grad_swap(block).wait_recv()
        grad_sel[block] = jnp.where(own_first, grad_own[block], grad_sib[block])

    def row_copy(side, k):
        way = 1 if side else -1
        return pltpu.make_async_remote_copy(
            src_ref=grad_sel.at[far_block(side, k)],
            dst_ref=request.at[side, pl.ds(k * height, height)],
            send_sem=row_send.at[side, k],
            recv_sem=row_recv.at[side, k],
            device_id=to(way * k),
            device_id_type=MESH,
        )

    grad_copy.wait()
    heard(2)
    last = 2
    for side, k in row_order:
        select_rows(far_block(side, k))
        while last < k:
            last += 1
            heard(last)
        row_copy(side, k).start()

    stat_copy.wait()
    stat_swap.wait_recv()
    pack(newton_root(jnp.where(own_first, stat_own[...], stat_sib[...])), own_root)

    def piece(c):
        return pl.ds(*pieces[c])

    def root_copy(side, d, c):
        source = own_root if d == 1 else roots.at[side, d - 2]
        return pltpu.make_async_remote_copy(
            src_ref=source.at[piece(c)],
            dst_ref=roots.at[side, d - 1, piece(c)],
            send_sem=root_send.at[side, d - 1, c],
            recv_sem=root_recv.at[side, d - 1, c],
            device_id=to(-1 if side else 1),
            device_id_type=MESH,
        )

    for c in range(chunks):
        for side in range(2):
            root_copy(side, 1, c).start()

    for d in range(-reach, reach + 1):
        select_rows(at(d))

    def columns(part):
        return pl.ds(part * half, half)

    def out_copies(slot, block, part):
        place = (block, slice(None), columns(part))
        local = pltpu.make_async_copy(
            result.at[place], out_ref.at[(0, *place)], out_local.at[part, slot]
        )
        remote = pltpu.make_async_remote_copy(
            src_ref=result.at[place],
            dst_ref=out_ref.at[(1, *place)],
            send_sem=out_send.at[part, slot],
            recv_sem=out_recv.at[part, slot],
            device_id=sibling,
            device_id_type=MESH,
        )
        return local, remote

    def out_slot(offset):
        return lax.rem(sign * offset + 4 * ring, ring)

    def send_out(offset, parts=(0, 1)):
        for part in parts:
            for copy in out_copies(out_slot(offset), at(offset), part):
                copy.start()

    result[me] = apply_root(grad_sel[me], own_root)
    send_out(0)

    for d in range(1, reach):
        for c in range(chunks):
            for side in range(2):
                root_copy(side, d, c).wait_recv()
                root_copy(side, d + 1, c).start()
        for side in range(2):
            offset = d if side else -d
            result[at(offset)] = apply_root(grad_sel[at(offset)], roots.at[side, d - 1])
            send_out(offset)

    def back_copy(side, k, part):
        way = 1 if side else -1
        return pltpu.make_async_remote_copy(
            src_ref=answer.at[side, part, pl.ds(k * height, height)],
            dst_ref=result.at[at(way * reach), :, columns(part)],
            send_sem=back_send.at[side, part, k],
            recv_sem=back_recv.at[side, part, k],
            device_id=to(-way * k),
            device_id_type=MESH,
        )

    def arrived(side, k, part):
        way = 1 if side else -1
        return pltpu.make_async_remote_copy(
            src_ref=answer.at[side, part, pl.ds(k * height, height)],
            dst_ref=result.at[at(way * (reach + k)), :, columns(part)],
            send_sem=back_send.at[side, part, k],
            recv_sem=back_recv.at[side, part, k],
            device_id=to(way * k),
            device_id_type=MESH,
        )

    served = [[k for s, k in far_sides if s == side] for side in range(2)]
    for side in (1, 0):
        for k in served[side]:
            row_copy(side, k).wait_recv()
        request[side, 0:height] = grad_sel[at((1 if side else -1) * reach)]
    for part, needed in ((0, range(chunks - 1)), (1, (chunks - 1,))):
        for side in (1, 0):
            offset = reach if side else -reach
            tall = (len(served[side]) + 1) * height
            for c in needed:
                root_copy(side, reach, c).wait_recv()
            product = (right_half if part else left_half)(request[side, 0:tall], roots.at[side, reach - 1])
            answer[side, part, 0:tall] = product
            for k in served[side]:
                back_copy(side, k, part).start()
            result[at(offset), :, part * half : (part + 1) * half] = product[0:height]
            send_out(offset, (part,))

    for part in range(2):
        for side, k in reversed(far_sides):
            arrived(side, k, part).wait_recv()
            send_out((1 if side else -1) * (reach + k), (part,))

    for offset in range(ring):
        grad_swap(lax.rem(me + offset, ring)).wait_send()
    stat_swap.wait_send()
    for side, k in far_sides:
        row_copy(side, k).wait_send()
        for part in range(2):
            back_copy(side, k, part).wait_send()
    for d in range(1, reach + 1):
        for c in range(chunks):
            for side in range(2):
                root_copy(side, d, c).wait_send()
    for offset in range(ring):
        for part in range(2):
            local, remote = out_copies(offset, lax.rem(me + offset, ring), part)
            local.wait()
            remote.wait()


def on_device(mesh, statistics, gradients, counts):
    ring = mesh.shape["mp"]
    reach = REACH
    slots, blocks, height, order = gradients.shape
    half = order // 2
    pieces = layout(half)[2]
    chunks, packed = len(pieces), sum(pieces[-1])
    tall = (ring // 2 - reach + 1) * height
    anywhere = pl.BlockSpec(memory_space=pl.ANY)
    in_hbm = pl.BlockSpec(memory_space=pltpu.HBM)
    dma = pltpu.SemaphoreType.DMA
    out = pl.pallas_call(
        functools.partial(kernel, ring, reach),
        out_shape=jax.ShapeDtypeStruct(gradients.shape, BF16),
        in_specs=[pl.BlockSpec(memory_space=pltpu.SMEM), in_hbm, in_hbm],
        out_specs=anywhere,
        scratch_shapes=[
            pltpu.VMEM((order, order), BF16),
            pltpu.VMEM((order, order), BF16),
            pltpu.VMEM((blocks, height, order), BF16),
            pltpu.VMEM((blocks, height, order), BF16),
            pltpu.VMEM((blocks, height, order), BF16),
            pltpu.VMEM((2, tall, order), BF16),
            pltpu.VMEM((2, 2, tall, half), BF16),
            pltpu.VMEM((packed, LANES), BF16),
            pltpu.VMEM((2, reach, packed, LANES), BF16),
            pltpu.VMEM((blocks, height, order), BF16),
            dma((2,)),
            dma((ring + 1,)),
            dma((ring + 1,)),
            dma((2, ring // 2)),
            dma((2, ring // 2)),
            dma((2, reach, chunks)),
            dma((2, reach, chunks)),
            dma((2, 2, ring // 2)),
            dma((2, 2, ring // 2)),
            dma((2, ring)),
            dma((2, ring)),
            dma((2, ring)),
            pltpu.SemaphoreType.REGULAR((2, ring // 2)),
        ],
        compiler_params=pltpu.CompilerParams(
            collective_id=0, has_side_effects=True, vmem_limit_bytes=52 * 1024 * 1024
        ),
        name="hybrid",
    )(counts, statistics, gradients)
    live = (jnp.arange(slots) < counts[0])[:, None, None, None]
    return jnp.where(live, out, jnp.zeros_like(out))


def solution(mesh):
    in_specs = (P("dp", "mp", None), P("dp", None, "mp", None), P("dp"))
    out_specs = P("dp", None, "mp", None)
    return jax.shard_map(
        functools.partial(on_device, mesh),
        mesh=mesh,
        in_specs=in_specs,
        out_specs=out_specs,
        check_vma=False,
    )
```

```python
import functools

import jax
import jax.numpy as jnp
from jax import lax
from jax.experimental import pallas as pl
from jax.experimental.pallas import tpu as pltpu
from jax.sharding import PartitionSpec as P

MESH = pl.DeviceIdType.MESH
LANES = 128
TAIL = 16
REACH = 4
RELAY = True
F32 = jnp.float32
BF16 = jnp.bfloat16


def dot(a, b):
    return jnp.dot(a, b, preferred_element_type=F32)


def dot_t(a, b):
    return lax.dot_general(a, b, (((1,), (1,)), ((), ())), preferred_element_type=F32)


def iotas(shape):
    return lax.broadcasted_iota(jnp.int32, shape, 0), lax.broadcasted_iota(jnp.int32, shape, 1)


def newton_root(block):
    order = block.shape[0]
    values = block.astype(F32)
    total = jnp.sum(jnp.sum(values * values, axis=1, keepdims=True), axis=0, keepdims=True)
    norm_scale = jnp.sqrt(total) + 1e-06
    scaled = (values * (1.0 / norm_scale)).astype(BF16)
    row, column = iotas((order, order))
    five = jnp.where(row == column, 5.0, 0.0).astype(F32)
    step_one = ((five - scaled.astype(F32)) * 0.25).astype(BF16)
    square = dot(step_one, step_one).astype(BF16)
    fourth = dot(square, square).astype(BF16)
    updated = dot(fourth, scaled)
    step_two = ((five - updated) * 0.25).astype(BF16)
    return dot(step_one, step_two) * lax.rsqrt(jnp.sqrt(norm_scale))


def layout(half):
    size = half * half // 2 // LANES
    lengths = [size, size + TAIL, size, size]
    return [(sum(lengths[:n]), lengths[n]) for n in range(len(lengths))]


def fold(block):
    size = block.shape[0] // 2
    row, column = iotas((size, size))
    corner = block[size:, size:]
    both = jnp.where(row <= column, block[:size, :size], corner)
    diagonal = jnp.sum(jnp.where(row == column, corner, 0.0), axis=0, keepdims=True)
    return block[:size, size:].astype(BF16), both.astype(BF16), diagonal


def unfold(above, both, diagonal):
    size = both.shape[0]
    row, column = iotas((size, size))
    both = both.astype(F32)
    mirror = both.T
    first = jnp.where(row <= column, both, mirror).astype(BF16)
    last = jnp.where(row > column, both, jnp.where(row == column, diagonal, mirror)).astype(BF16)
    below = above.astype(F32).T.astype(BF16)
    return jnp.concatenate(
        [jnp.concatenate([first, above], axis=1), jnp.concatenate([below, last], axis=1)], axis=0
    )


def store_slabs(ref, start, block):
    height, width = block.shape
    for j in range(width // LANES):
        ref[start + j * height : start + (j + 1) * height, :] = block[:, j * LANES : (j + 1) * LANES]
    return start + height * width // LANES


def load_slabs(ref, start, height, width):
    slabs = [ref[start + j * height : start + (j + 1) * height, :] for j in range(width // LANES)]
    return jnp.concatenate(slabs, axis=1) if len(slabs) > 1 else slabs[0]


def pack(root, ref):
    half = root.shape[0] // 2
    size = half // 2
    starts = [start for start, _ in layout(half)]
    across = root[:half, half:].astype(BF16)
    above_0, both_0, diagonal_0 = fold(root[:half, :half])
    above_1, both_1, diagonal_1 = fold(root[half:, half:])
    store_slabs(ref, starts[0], across[:size])
    end = store_slabs(ref, store_slabs(ref, starts[1], above_0), both_0)
    tail_row, _ = iotas((TAIL, size))
    tail = jnp.where(tail_row == 0, diagonal_0, jnp.where(tail_row == 1, diagonal_1, 0.0))
    ref[end : end + TAIL, :] = tail.astype(BF16)
    store_slabs(ref, starts[2], across[size:])
    store_slabs(ref, store_slabs(ref, starts[3], above_1), both_1)


def unpack_across(ref, half, which):
    return load_slabs(ref, layout(half)[2 * which][0], half // 2, half)


def unpack_corner(ref, half, which):
    size = half // 2
    starts = [start for start, _ in layout(half)]
    start = starts[1 + 2 * which]
    above = load_slabs(ref, start, size, size)
    both = load_slabs(ref, start + size * size // LANES, size, size)
    tail = ref[starts[2] - TAIL : starts[2], :].astype(F32)
    return unfold(above, both, tail[which : which + 1, :])


def apply_part(rows, ref, part):
    half = rows.shape[1] // 2
    size = half // 2
    left, right = rows[:, :half], rows[:, half:]
    if part < 2:
        corner = unpack_corner(ref, half, 0)[:, part * size : (part + 1) * size]
        return (dot(left, corner) + dot_t(right, unpack_across(ref, half, part))).astype(BF16)
    across = jnp.concatenate([unpack_across(ref, half, 0), unpack_across(ref, half, 1)], axis=0)
    return (dot(left, across) + dot(right, unpack_corner(ref, half, 1))).astype(BF16)


def apply_root(rows, ref):
    half = rows.shape[1] // 2
    left, right = rows[:, :half], rows[:, half:]
    across = jnp.concatenate([unpack_across(ref, half, 0), unpack_across(ref, half, 1)], axis=0)
    out_left = dot(left, unpack_corner(ref, half, 0)) + dot_t(right, across)
    out_right = dot(left, across) + dot(right, unpack_corner(ref, half, 1))
    return jnp.concatenate([out_left, out_right], axis=1).astype(BF16)


def kernel(
    ring,
    reach,
    counts_ref,
    stat_ref,
    grad_ref,
    out_ref,
    stat_own,
    stat_sib,
    grad_own,
    grad_sib,
    grad_sel,
    request,
    answer,
    own_root,
    roots,
    result,
    local_sem,
    sib_send,
    sib_recv,
    row_send,
    row_recv,
    root_send,
    root_recv,
    back_send,
    back_recv,
    out_sem,
    ready,
):
    dp, me = lax.axis_index("dp"), lax.axis_index("mp")
    core = lax.rem(dp, 2)
    sibling = {"dp": dp + 1 - 2 * core}
    sign = 1 - 2 * core
    order = stat_own.shape[0]
    half = order // 2
    pieces = layout(half)
    chunks = len(pieces)
    parts = [(0, half // 2), (half // 2, half // 2), (half, half)]
    height = grad_own.shape[1]

    def at(offset):
        return lax.rem(me + sign * offset + 4 * ring, ring)

    def to(offset):
        return {"mp": at(offset)}

    stat_copy = pltpu.make_async_copy(stat_ref.at[0], stat_own, local_sem.at[0])
    grad_copy = pltpu.make_async_copy(grad_ref.at[0], grad_own, local_sem.at[1])
    grad_copy.start()
    stat_copy.start()

    barrier = pltpu.get_barrier_semaphore()
    pl.semaphore_signal(barrier, inc=1, device_id=sibling, device_id_type=MESH)
    span = max(1, ring // 2 - reach)
    direct = 1 if RELAY else span
    for d in range(1, direct + 1):
        pl.semaphore_signal(barrier, inc=1, device_id=to(d), device_id_type=MESH)
        pl.semaphore_signal(barrier, inc=1, device_id=to(-d), device_id_type=MESH)
    pl.semaphore_wait(barrier, 2 * direct + 1)

    def tell(d):
        if RELAY and d <= span:
            pl.semaphore_signal(ready.at[0, d], inc=1, device_id=to(1), device_id_type=MESH)
            pl.semaphore_signal(ready.at[1, d], inc=1, device_id=to(-1), device_id_type=MESH)

    def heard(d):
        if RELAY and 1 < d <= span:
            pl.semaphore_wait(ready.at[0, d], 1)
            pl.semaphore_wait(ready.at[1, d], 1)
            tell(d + 1)

    tell(2)

    def grad_swap(block):
        j = lax.rem(block - me + ring, ring)
        return pltpu.make_async_remote_copy(
            src_ref=grad_ref.at[1, block],
            dst_ref=grad_sib.at[block],
            send_sem=sib_send.at[0],
            recv_sem=sib_recv.at[j],
            device_id=sibling,
            device_id_type=MESH,
        )

    stat_swap = pltpu.make_async_remote_copy(
        src_ref=stat_ref.at[1],
        dst_ref=stat_sib,
        send_sem=sib_send.at[1],
        recv_sem=sib_recv.at[ring],
        device_id=sibling,
        device_id_type=MESH,
    )
    far_sides = [(1, ring // 2 - reach)]
    for k in range(ring // 2 - reach - 1, 0, -1):
        far_sides += [(1, k), (0, k)]
    nearest_first = far_sides[::-1]
    row_order = nearest_first if RELAY else far_sides

    def far_block(side, k):
        return at((1 if side else -1) * (reach + k))

    for side, k in row_order:
        grad_swap(far_block(side, k)).start()
    stat_swap.start()
    for d in range(-reach, reach + 1):
        grad_swap(at(d)).start()

    own_first = counts_ref[0] >= 1

    def select_rows(block):
        grad_swap(block).wait_recv()
        grad_sel[block] = jnp.where(own_first, grad_own[block], grad_sib[block])

    def row_copy(side, k):
        way = 1 if side else -1
        return pltpu.make_async_remote_copy(
            src_ref=grad_sel.at[far_block(side, k)],
            dst_ref=request.at[side, pl.ds(k * height, height)],
            send_sem=row_send.at[0],
            recv_sem=row_recv.at[side, k],
            device_id=to(way * k),
            device_id_type=MESH,
        )

    grad_copy.wait()
    heard(2)
    last = 2
    for side, k in row_order:
        select_rows(far_block(side, k))
        while last < k:
            last += 1
            heard(last)
        row_copy(side, k).start()

    stat_copy.wait()
    stat_swap.wait_recv()
    pack(newton_root(jnp.where(own_first, stat_own[...], stat_sib[...])), own_root)

    def piece(c):
        return pl.ds(*pieces[c])

    def root_copy(side, d, c):
        source = own_root if d == 1 else roots.at[side, d - 2]
        return pltpu.make_async_remote_copy(
            src_ref=source.at[piece(c)],
            dst_ref=roots.at[side, d - 1, piece(c)],
            send_sem=root_send.at[0],
            recv_sem=root_recv.at[side, d - 1, c],
            device_id=to(-1 if side else 1),
            device_id_type=MESH,
        )

    for c in range(chunks):
        for side in range(2):
            root_copy(side, 1, c).start()

    for d in range(-reach, reach + 1):
        select_rows(at(d))

    def out_copies(source, own, other):
        local = pltpu.make_async_copy(source, own, out_sem.at[0])
        remote = pltpu.make_async_remote_copy(
            src_ref=source,
            dst_ref=other,
            send_sem=out_sem.at[1],
            recv_sem=out_sem.at[2],
            device_id=sibling,
            device_id_type=MESH,
        )
        return local, remote

    def send_out(offset, start=0, width=order):
        place = (at(offset), slice(None), pl.ds(start, width))
        for copy in out_copies(result.at[place], out_ref.at[(0, *place)], out_ref.at[(1, *place)]):
            copy.start()

    result[me] = apply_root(grad_sel[me], own_root)
    send_out(0)

    for d in range(1, reach):
        for c in range(chunks):
            for side in range(2):
                root_copy(side, d, c).wait_recv()
                root_copy(side, d + 1, c).start()
        for side in range(2):
            offset = d if side else -d
            result[at(offset)] = apply_root(grad_sel[at(offset)], roots.at[side, d - 1])
            send_out(offset)

    def back_copy(side, k, part):
        way = 1 if side else -1
        return pltpu.make_async_remote_copy(
            src_ref=answer.at[side, pl.ds(k * height, height), pl.ds(*parts[part])],
            dst_ref=result.at[at(way * reach), :, pl.ds(*parts[part])],
            send_sem=back_send.at[0],
            recv_sem=back_recv.at[side, part, k],
            device_id=to(-way * k),
            device_id_type=MESH,
        )

    def arrived(side, k, part):
        way = 1 if side else -1
        return pltpu.make_async_remote_copy(
            src_ref=answer.at[side, pl.ds(k * height, height), pl.ds(*parts[part])],
            dst_ref=result.at[at(way * (reach + k)), :, pl.ds(*parts[part])],
            send_sem=back_send.at[0],
            recv_sem=back_recv.at[side, part, k],
            device_id=to(way * k),
            device_id_type=MESH,
        )

    served = [[k for s, k in far_sides if s == side] for side in range(2)]
    for side in (1, 0):
        for k in served[side]:
            row_copy(side, k).wait_recv()
    for part, needed in ((0, (0, 1)), (1, (2,)), (2, (3,))):
        for side in (1, 0):
            rows = slice(height, (len(served[side]) + 1) * height)
            start, width = parts[part]
            for c in needed:
                root_copy(side, reach, c).wait_recv()
            answer[side, rows, start : start + width] = apply_part(
                request[side, rows], roots.at[side, reach - 1], part
            )
            for k in served[side]:
                back_copy(side, k, part).start()
    for side in (1, 0):
        offset = reach if side else -reach
        result[at(offset)] = apply_root(grad_sel[at(offset)], roots.at[side, reach - 1])
        send_out(offset)

    def all_sent(source, sem):
        pltpu.make_async_remote_copy(
            src_ref=source,
            dst_ref=source,
            send_sem=sem,
            recv_sem=sib_recv.at[0],
            device_id=sibling,
            device_id_type=MESH,
        ).wait_send()

    all_sent(grad_sib, sib_send.at[0])
    all_sent(stat_sib, sib_send.at[1])
    all_sent(grad_sel.at[pl.ds(0, len(far_sides))], row_send.at[0])
    all_sent(roots, root_send.at[0])

    for part in range(3):
        for side, k in far_sides:
            arrived(side, k, part).wait_recv()
            if part > 0:
                send_out((1 if side else -1) * (reach + k), (part - 1) * half, half)

    all_sent(grad_sel.at[pl.ds(0, len(far_sides))], back_send.at[0])
    for copy in out_copies(result, out_ref.at[0], out_ref.at[1]):
        copy.wait()


def on_device(mesh, statistics, gradients, counts):
    ring = mesh.shape["mp"]
    reach = REACH
    slots, blocks, height, order = gradients.shape
    half = order // 2
    pieces = layout(half)
    chunks, packed = len(pieces), sum(pieces[-1])
    tall = (ring // 2 - reach + 1) * height
    anywhere = pl.BlockSpec(memory_space=pl.ANY)
    in_hbm = pl.BlockSpec(memory_space=pltpu.HBM)
    dma = pltpu.SemaphoreType.DMA
    out = pl.pallas_call(
        functools.partial(kernel, ring, reach),
        out_shape=jax.ShapeDtypeStruct(gradients.shape, BF16),
        in_specs=[pl.BlockSpec(memory_space=pltpu.SMEM), in_hbm, in_hbm],
        out_specs=anywhere,
        scratch_shapes=[
            pltpu.VMEM((order, order), BF16),
            pltpu.VMEM((order, order), BF16),
            pltpu.VMEM((blocks, height, order), BF16),
            pltpu.VMEM((blocks, height, order), BF16),
            pltpu.VMEM((blocks, height, order), BF16),
            pltpu.VMEM((2, tall, order), BF16),
            pltpu.VMEM((2, tall, order), BF16),
            pltpu.VMEM((packed, LANES), BF16),
            pltpu.VMEM((2, reach, packed, LANES), BF16),
            pltpu.VMEM((blocks, height, order), BF16),
            dma((2,)),
            dma((2,)),
            dma((ring + 1,)),
            dma((1,)),
            dma((2, ring // 2)),
            dma((1,)),
            dma((2, reach, chunks)),
            dma((1,)),
            dma((2, 3, ring // 2)),
            dma((3,)),
            pltpu.SemaphoreType.REGULAR((2, ring // 2)),
        ],
        compiler_params=pltpu.CompilerParams(
            collective_id=0, has_side_effects=True, vmem_limit_bytes=52 * 1024 * 1024
        ),
        name="hybrid",
    )(counts, statistics, gradients)
    live = (jnp.arange(slots) < counts[0])[:, None, None, None]
    return jnp.where(live, out, jnp.zeros_like(out))


def solution(mesh):
    in_specs = (P("dp", "mp", None), P("dp", None, "mp", None), P("dp"))
    out_specs = P("dp", None, "mp", None)
    return jax.shard_map(
        functools.partial(on_device, mesh),
        mesh=mesh,
        in_specs=in_specs,
        out_specs=out_specs,
        check_vma=False,
    )
```

```python
import functools

import jax
import jax.numpy as jnp
from jax import lax
from jax.experimental import pallas as pl
from jax.experimental.pallas import tpu as pltpu
from jax.sharding import PartitionSpec as P

MESH = pl.DeviceIdType.MESH
LANES = 128
TAIL = 16
REACH = 4
RELAY = True
F32 = jnp.float32
BF16 = jnp.bfloat16


def dot(a, b):
    return jnp.dot(a, b, preferred_element_type=F32)


def dot_t(a, b):
    return lax.dot_general(a, b, (((1,), (1,)), ((), ())), preferred_element_type=F32)


def iotas(shape):
    return lax.broadcasted_iota(jnp.int32, shape, 0), lax.broadcasted_iota(jnp.int32, shape, 1)


def newton_root(block):
    order = block.shape[0]
    values = block.astype(F32)
    total = jnp.sum(jnp.sum(values * values, axis=1, keepdims=True), axis=0, keepdims=True)
    norm_scale = jnp.sqrt(total) + 1e-06
    scaled = (values * (1.0 / norm_scale)).astype(BF16)
    row, column = iotas((order, order))
    five = jnp.where(row == column, 5.0, 0.0).astype(F32)
    step_one = ((five - scaled.astype(F32)) * 0.25).astype(BF16)
    square = dot(step_one, step_one).astype(BF16)
    fourth = dot(square, square).astype(BF16)
    updated = dot(fourth, scaled)
    step_two = ((five - updated) * 0.25).astype(BF16)
    return dot(step_one, step_two) * lax.rsqrt(jnp.sqrt(norm_scale))


def layout(half):
    size = half * half // 2 // LANES
    lengths = [size, size + TAIL, size, size]
    return [(sum(lengths[:n]), lengths[n]) for n in range(len(lengths))]


def fold(block):
    size = block.shape[0] // 2
    row, column = iotas((size, size))
    corner = block[size:, size:]
    both = jnp.where(row <= column, block[:size, :size], corner)
    diagonal = jnp.sum(jnp.where(row == column, corner, 0.0), axis=0, keepdims=True)
    return block[:size, size:].astype(BF16), both.astype(BF16), diagonal


def unfold(above, both, diagonal):
    size = both.shape[0]
    row, column = iotas((size, size))
    both = both.astype(F32)
    mirror = both.T
    first = jnp.where(row <= column, both, mirror).astype(BF16)
    last = jnp.where(row > column, both, jnp.where(row == column, diagonal, mirror)).astype(BF16)
    below = above.astype(F32).T.astype(BF16)
    return jnp.concatenate(
        [jnp.concatenate([first, above], axis=1), jnp.concatenate([below, last], axis=1)], axis=0
    )


def store_slabs(ref, start, block):
    height, width = block.shape
    for j in range(width // LANES):
        ref[start + j * height : start + (j + 1) * height, :] = block[:, j * LANES : (j + 1) * LANES]
    return start + height * width // LANES


def load_slabs(ref, start, height, width):
    slabs = [ref[start + j * height : start + (j + 1) * height, :] for j in range(width // LANES)]
    return jnp.concatenate(slabs, axis=1) if len(slabs) > 1 else slabs[0]


def pack(root, ref):
    half = root.shape[0] // 2
    size = half // 2
    starts = [start for start, _ in layout(half)]
    across = root[:half, half:].astype(BF16)
    above_0, both_0, diagonal_0 = fold(root[:half, :half])
    above_1, both_1, diagonal_1 = fold(root[half:, half:])
    store_slabs(ref, starts[0], across[:size])
    end = store_slabs(ref, store_slabs(ref, starts[1], above_0), both_0)
    tail_row, _ = iotas((TAIL, size))
    tail = jnp.where(tail_row == 0, diagonal_0, jnp.where(tail_row == 1, diagonal_1, 0.0))
    ref[end : end + TAIL, :] = tail.astype(BF16)
    store_slabs(ref, starts[2], across[size:])
    store_slabs(ref, store_slabs(ref, starts[3], above_1), both_1)


def unpack_across(ref, half, which):
    return load_slabs(ref, layout(half)[2 * which][0], half // 2, half)


def unpack_corner(ref, half, which):
    size = half // 2
    starts = [start for start, _ in layout(half)]
    start = starts[1 + 2 * which]
    above = load_slabs(ref, start, size, size)
    both = load_slabs(ref, start + size * size // LANES, size, size)
    tail = ref[starts[2] - TAIL : starts[2], :].astype(F32)
    return unfold(above, both, tail[which : which + 1, :])


def apply_part(rows, ref, part):
    half = rows.shape[1] // 2
    size = half // 2
    left, right = rows[:, :half], rows[:, half:]
    if part < 2:
        corner = unpack_corner(ref, half, 0)[:, part * size : (part + 1) * size]
        return (dot(left, corner) + dot_t(right, unpack_across(ref, half, part))).astype(BF16)
    across = jnp.concatenate([unpack_across(ref, half, 0), unpack_across(ref, half, 1)], axis=0)
    return (dot(left, across) + dot(right, unpack_corner(ref, half, 1))).astype(BF16)


def apply_root(rows, ref):
    half = rows.shape[1] // 2
    left, right = rows[:, :half], rows[:, half:]
    across = jnp.concatenate([unpack_across(ref, half, 0), unpack_across(ref, half, 1)], axis=0)
    out_left = dot(left, unpack_corner(ref, half, 0)) + dot_t(right, across)
    out_right = dot(left, across) + dot(right, unpack_corner(ref, half, 1))
    return jnp.concatenate([out_left, out_right], axis=1).astype(BF16)


def kernel(
    ring,
    reach,
    counts_ref,
    stat_ref,
    grad_ref,
    out_ref,
    stat_own,
    stat_sib,
    grad_own,
    grad_sib,
    grad_sel,
    request,
    answer,
    own_root,
    roots,
    result,
    local_sem,
    sib_send,
    sib_recv,
    row_send,
    row_recv,
    root_send,
    root_recv,
    back_send,
    back_recv,
    out_sem,
    ready,
):
    dp, me = lax.axis_index("dp"), lax.axis_index("mp")
    core = lax.rem(dp, 2)
    sibling = {"dp": dp + 1 - 2 * core}
    sign = 1 - 2 * core
    order = stat_own.shape[0]
    half = order // 2
    pieces = layout(half)
    chunks = len(pieces)
    parts = [(0, half // 2), (half // 2, half // 2), (half, half)]
    height = grad_own.shape[1]

    def at(offset):
        return lax.rem(me + sign * offset + 4 * ring, ring)

    def to(offset):
        return {"mp": at(offset)}

    stat_copy = pltpu.make_async_copy(stat_ref.at[0], stat_own, local_sem.at[0])
    grad_copy = pltpu.make_async_copy(grad_ref.at[0], grad_own, local_sem.at[1])
    grad_copy.start()
    stat_copy.start()

    barrier = pltpu.get_barrier_semaphore()
    pl.semaphore_signal(barrier, inc=1, device_id=sibling, device_id_type=MESH)
    span = max(1, ring // 2 - reach)
    direct = 1 if RELAY else span
    for d in range(1, direct + 1):
        pl.semaphore_signal(barrier, inc=1, device_id=to(d), device_id_type=MESH)
        pl.semaphore_signal(barrier, inc=1, device_id=to(-d), device_id_type=MESH)
    pl.semaphore_wait(barrier, 2 * direct + 1)

    def tell(d):
        if RELAY and d <= span:
            pl.semaphore_signal(ready.at[0, d], inc=1, device_id=to(1), device_id_type=MESH)
            pl.semaphore_signal(ready.at[1, d], inc=1, device_id=to(-1), device_id_type=MESH)

    def heard(d):
        if RELAY and 1 < d <= span:
            pl.semaphore_wait(ready.at[0, d], 1)
            pl.semaphore_wait(ready.at[1, d], 1)
            tell(d + 1)

    tell(2)

    def grad_swap(block, near=False):
        j = 0 if near else lax.rem(block - me + ring, ring)
        return pltpu.make_async_remote_copy(
            src_ref=grad_ref.at[1, block],
            dst_ref=grad_sib.at[block],
            send_sem=sib_send.at[0],
            recv_sem=sib_recv.at[j],
            device_id=sibling,
            device_id_type=MESH,
        )

    stat_swap = pltpu.make_async_remote_copy(
        src_ref=stat_ref.at[1],
        dst_ref=stat_sib,
        send_sem=sib_send.at[1],
        recv_sem=sib_recv.at[1],
        device_id=sibling,
        device_id_type=MESH,
    )
    far_sides = [(1, ring // 2 - reach)]
    for k in range(ring // 2 - reach - 1, 0, -1):
        far_sides += [(1, k), (0, k)]
    nearest_first = far_sides[::-1]
    row_order = nearest_first if RELAY else far_sides

    def far_block(side, k):
        return at((1 if side else -1) * (reach + k))

    for side, k in row_order:
        grad_swap(far_block(side, k)).start()
    stat_swap.start()
    for d in range(-reach, reach + 1):
        grad_swap(at(d), near=True).start()

    own_first = counts_ref[0] >= 1

    def select_rows(block):
        grad_sel[block] = jnp.where(own_first, grad_own[block], grad_sib[block])

    def row_copy(side, k):
        way = 1 if side else -1
        return pltpu.make_async_remote_copy(
            src_ref=grad_sel.at[far_block(side, k)],
            dst_ref=request.at[side, pl.ds(k * height, height)],
            send_sem=row_send.at[0],
            recv_sem=row_recv.at[0],
            device_id=to(way * k),
            device_id_type=MESH,
        )

    grad_copy.wait()
    heard(2)
    last = 2
    for side, k in row_order:
        grad_swap(far_block(side, k)).wait_recv()
        select_rows(far_block(side, k))
        while last < k:
            last += 1
            heard(last)
        row_copy(side, k).start()

    stat_copy.wait()
    stat_swap.wait_recv()
    pack(newton_root(jnp.where(own_first, stat_own[...], stat_sib[...])), own_root)

    def piece(c):
        return pl.ds(*pieces[c])

    def root_copy(side, d, c):
        source = own_root if d == 1 else roots.at[side, d - 2]
        return pltpu.make_async_remote_copy(
            src_ref=source.at[piece(c)],
            dst_ref=roots.at[side, d - 1, piece(c)],
            send_sem=root_send.at[0],
            recv_sem=root_recv.at[side, d - 1, c],
            device_id=to(-1 if side else 1),
            device_id_type=MESH,
        )

    for c in range(chunks):
        for side in range(2):
            root_copy(side, 1, c).start()

    def all_here(place, sem):
        pltpu.make_async_remote_copy(
            src_ref=place,
            dst_ref=place,
            send_sem=sib_send.at[0],
            recv_sem=sem,
            device_id=sibling,
            device_id_type=MESH,
        ).wait_recv()

    all_here(grad_sib.at[pl.ds(0, 2 * reach + 1)], sib_recv.at[0])
    for d in range(-reach, reach + 1):
        select_rows(at(d))

    def out_copies(source, own, other):
        local = pltpu.make_async_copy(source, own, out_sem.at[0])
        remote = pltpu.make_async_remote_copy(
            src_ref=source,
            dst_ref=other,
            send_sem=out_sem.at[1],
            recv_sem=out_sem.at[2],
            device_id=sibling,
            device_id_type=MESH,
        )
        return local, remote

    def send_out(offset, start=0, width=order):
        place = (at(offset), slice(None), pl.ds(start, width))
        for copy in out_copies(result.at[place], out_ref.at[(0, *place)], out_ref.at[(1, *place)]):
            copy.start()

    result[me] = apply_root(grad_sel[me], own_root)
    send_out(0)

    for d in range(1, reach):
        for c in range(chunks):
            for side in range(2):
                root_copy(side, d, c).wait_recv()
                root_copy(side, d + 1, c).start()
        for side in range(2):
            offset = d if side else -d
            result[at(offset)] = apply_root(grad_sel[at(offset)], roots.at[side, d - 1])
            send_out(offset)

    def back_copy(side, k, part):
        way = 1 if side else -1
        return pltpu.make_async_remote_copy(
            src_ref=answer.at[side, pl.ds(k * height, height), pl.ds(*parts[part])],
            dst_ref=result.at[at(way * reach), :, pl.ds(*parts[part])],
            send_sem=back_send.at[0],
            recv_sem=back_recv.at[side, k if part == 2 else 0],
            device_id=to(-way * k),
            device_id_type=MESH,
        )

    def arrived(side, k, part):
        way = 1 if side else -1
        return pltpu.make_async_remote_copy(
            src_ref=answer.at[side, pl.ds(k * height, height), pl.ds(*parts[part])],
            dst_ref=result.at[at(way * (reach + k)), :, pl.ds(*parts[part])],
            send_sem=back_send.at[0],
            recv_sem=back_recv.at[side, k if part == 2 else 0],
            device_id=to(way * k),
            device_id_type=MESH,
        )

    served = [[k for s, k in far_sides if s == side] for side in range(2)]
    all_here(grad_sel.at[pl.ds(0, len(far_sides))], row_recv.at[0])
    for part, needed in ((0, (0, 1)), (1, (2,)), (2, (3,))):
        for side in (1, 0):
            rows = slice(height, (len(served[side]) + 1) * height)
            start, width = parts[part]
            for c in needed:
                root_copy(side, reach, c).wait_recv()
            answer[side, rows, start : start + width] = apply_part(
                request[side, rows], roots.at[side, reach - 1], part
            )
            for k in served[side]:
                back_copy(side, k, part).start()
    for side in (1, 0):
        offset = reach if side else -reach
        result[at(offset)] = apply_root(grad_sel[at(offset)], roots.at[side, reach - 1])
        send_out(offset)

    def all_sent(source, sem):
        pltpu.make_async_remote_copy(
            src_ref=source,
            dst_ref=source,
            send_sem=sem,
            recv_sem=sib_recv.at[0],
            device_id=sibling,
            device_id_type=MESH,
        ).wait_send()

    all_sent(grad_sib, sib_send.at[0])
    all_sent(stat_sib, sib_send.at[1])
    all_sent(grad_sel.at[pl.ds(0, len(far_sides))], row_send.at[0])
    all_sent(roots, root_send.at[0])

    for side in range(2):
        all_here(answer.at[side, pl.ds(0, len(served[side]) * height), pl.ds(0, half)], back_recv.at[side, 0])
    for side, k in far_sides:
        send_out((1 if side else -1) * (reach + k), 0, half)
    for side, k in far_sides:
        arrived(side, k, 2).wait_recv()
        send_out((1 if side else -1) * (reach + k), half, half)
    all_sent(grad_sel.at[pl.ds(0, len(far_sides))], back_send.at[0])
    for copy in out_copies(result, out_ref.at[0], out_ref.at[1]):
        copy.wait()


def on_device(mesh, statistics, gradients, counts):
    ring = mesh.shape["mp"]
    reach = REACH
    slots, blocks, height, order = gradients.shape
    half = order // 2
    pieces = layout(half)
    chunks, packed = len(pieces), sum(pieces[-1])
    tall = (ring // 2 - reach + 1) * height
    anywhere = pl.BlockSpec(memory_space=pl.ANY)
    in_hbm = pl.BlockSpec(memory_space=pltpu.HBM)
    dma = pltpu.SemaphoreType.DMA
    out = pl.pallas_call(
        functools.partial(kernel, ring, reach),
        out_shape=jax.ShapeDtypeStruct(gradients.shape, BF16),
        in_specs=[pl.BlockSpec(memory_space=pltpu.SMEM), in_hbm, in_hbm],
        out_specs=anywhere,
        scratch_shapes=[
            pltpu.VMEM((order, order), BF16),
            pltpu.VMEM((order, order), BF16),
            pltpu.VMEM((blocks, height, order), BF16),
            pltpu.VMEM((blocks, height, order), BF16),
            pltpu.VMEM((blocks, height, order), BF16),
            pltpu.VMEM((2, tall, order), BF16),
            pltpu.VMEM((2, tall, order), BF16),
            pltpu.VMEM((packed, LANES), BF16),
            pltpu.VMEM((2, reach, packed, LANES), BF16),
            pltpu.VMEM((blocks, height, order), BF16),
            dma((2,)),
            dma((2,)),
            dma((ring - reach,)),
            dma((1,)),
            dma((1,)),
            dma((1,)),
            dma((2, reach, chunks)),
            dma((1,)),
            dma((2, ring // 2 - reach + 1)),
            dma((3,)),
            pltpu.SemaphoreType.REGULAR((2, ring // 2 - reach + 1)),
        ],
        compiler_params=pltpu.CompilerParams(
            collective_id=0, has_side_effects=True, vmem_limit_bytes=52 * 1024 * 1024
        ),
        name="hybrid",
    )(counts, statistics, gradients)
    live = (jnp.arange(slots) < counts[0])[:, None, None, None]
    return jnp.where(live, out, jnp.zeros_like(out))


def solution(mesh):
    in_specs = (P("dp", "mp", None), P("dp", None, "mp", None), P("dp"))
    out_specs = P("dp", None, "mp", None)
    return jax.shard_map(
        functools.partial(on_device, mesh),
        mesh=mesh,
        in_specs=in_specs,
        out_specs=out_specs,
        check_vma=False,
    )
```

```python
import functools

import jax
import jax.numpy as jnp
from jax import lax
from jax.experimental import pallas as pl
from jax.experimental.pallas import tpu as pltpu
from jax.sharding import PartitionSpec as P

MESH = pl.DeviceIdType.MESH
LANES = 128
TAIL = 16
CUTS = 4
REACH = 4
RELAY = True
F32 = jnp.float32
BF16 = jnp.bfloat16


def dot(a, b):
    return jnp.dot(a, b, preferred_element_type=F32)


def dot_t(a, b):
    return lax.dot_general(a, b, (((1,), (1,)), ((), ())), preferred_element_type=F32)


def iotas(shape):
    return lax.broadcasted_iota(jnp.int32, shape, 0), lax.broadcasted_iota(jnp.int32, shape, 1)


def newton_root(block):
    order = block.shape[0]
    values = block.astype(F32)
    total = jnp.sum(jnp.sum(values * values, axis=1, keepdims=True), axis=0, keepdims=True)
    norm_scale = jnp.sqrt(total) + 1e-06
    scaled = (values * (1.0 / norm_scale)).astype(BF16)
    row, column = iotas((order, order))
    five = jnp.where(row == column, 5.0, 0.0).astype(F32)
    step_one = ((five - scaled.astype(F32)) * 0.25).astype(BF16)
    square = dot(step_one, step_one).astype(BF16)
    fourth = dot(square, square).astype(BF16)
    updated = dot(fourth, scaled)
    step_two = ((five - updated) * 0.25).astype(BF16)
    return dot(step_one, step_two) * lax.rsqrt(jnp.sqrt(norm_scale))


def layout(half):
    size = half * half // 2 // LANES
    lengths = [size, size + TAIL, size, size]
    return [(sum(lengths[:n]), lengths[n]) for n in range(len(lengths))]


def fold(block):
    size = block.shape[0] // 2
    row, column = iotas((size, size))
    corner = block[size:, size:]
    both = jnp.where(row <= column, block[:size, :size], corner)
    diagonal = jnp.sum(jnp.where(row == column, corner, 0.0), axis=0, keepdims=True)
    return block[:size, size:].astype(BF16), both.astype(BF16), diagonal


def unfold(above, both, diagonal):
    size = both.shape[0]
    row, column = iotas((size, size))
    both = both.astype(F32)
    mirror = both.T
    first = jnp.where(row <= column, both, mirror).astype(BF16)
    last = jnp.where(row > column, both, jnp.where(row == column, diagonal, mirror)).astype(BF16)
    below = above.astype(F32).T.astype(BF16)
    return jnp.concatenate(
        [jnp.concatenate([first, above], axis=1), jnp.concatenate([below, last], axis=1)], axis=0
    )


def store_slabs(ref, start, block):
    height, width = block.shape
    for j in range(width // LANES):
        ref[start + j * height : start + (j + 1) * height, :] = block[:, j * LANES : (j + 1) * LANES]
    return start + height * width // LANES


def load_slabs(ref, start, height, width):
    slabs = [ref[start + j * height : start + (j + 1) * height, :] for j in range(width // LANES)]
    return jnp.concatenate(slabs, axis=1) if len(slabs) > 1 else slabs[0]


def pack(root, ref):
    half = root.shape[0] // 2
    size = half // 2
    starts = [start for start, _ in layout(half)]
    across = root[:half, half:].astype(BF16)
    above_0, both_0, diagonal_0 = fold(root[:half, :half])
    above_1, both_1, diagonal_1 = fold(root[half:, half:])
    store_slabs(ref, starts[0], across[:size])
    end = store_slabs(ref, store_slabs(ref, starts[1], above_0), both_0)
    tail_row, _ = iotas((TAIL, size))
    tail = jnp.where(tail_row == 0, diagonal_0, jnp.where(tail_row == 1, diagonal_1, 0.0))
    ref[end : end + TAIL, :] = tail.astype(BF16)
    store_slabs(ref, starts[2], across[size:])
    store_slabs(ref, store_slabs(ref, starts[3], above_1), both_1)


def unpack_across(ref, half, which):
    return load_slabs(ref, layout(half)[2 * which][0], half // 2, half)


def unpack_corner(ref, half, which):
    size = half // 2
    starts = [start for start, _ in layout(half)]
    start = starts[1 + 2 * which]
    above = load_slabs(ref, start, size, size)
    both = load_slabs(ref, start + size * size // LANES, size, size)
    tail = ref[starts[2] - TAIL : starts[2], :].astype(F32)
    return unfold(above, both, tail[which : which + 1, :])


def apply_part(rows, ref, part):
    half = rows.shape[1] // 2
    size = half // 2
    left, right = rows[:, :half], rows[:, half:]
    if part < 2:
        corner = unpack_corner(ref, half, 0)[:, part * size : (part + 1) * size]
        return (dot(left, corner) + dot_t(right, unpack_across(ref, half, part))).astype(BF16)
    across = jnp.concatenate([unpack_across(ref, half, 0), unpack_across(ref, half, 1)], axis=0)
    return (dot(left, across) + dot(right, unpack_corner(ref, half, 1))).astype(BF16)


def apply_root(rows, ref):
    half = rows.shape[1] // 2
    left, right = rows[:, :half], rows[:, half:]
    across = jnp.concatenate([unpack_across(ref, half, 0), unpack_across(ref, half, 1)], axis=0)
    out_left = dot(left, unpack_corner(ref, half, 0)) + dot_t(right, across)
    out_right = dot(left, across) + dot(right, unpack_corner(ref, half, 1))
    return jnp.concatenate([out_left, out_right], axis=1).astype(BF16)


def kernel(
    ring,
    reach,
    counts_ref,
    stat_ref,
    grad_ref,
    out_ref,
    stat_own,
    stat_sib,
    grad_own,
    grad_sib,
    grad_sel,
    request,
    answer,
    own_root,
    roots,
    result,
    local_sem,
    sib_send,
    sib_recv,
    row_send,
    row_recv,
    root_send,
    root_recv,
    back_send,
    back_recv,
    out_sem,
    ready,
):
    dp, me = lax.axis_index("dp"), lax.axis_index("mp")
    core = lax.rem(dp, 2)
    sibling = {"dp": dp + 1 - 2 * core}
    sign = 1 - 2 * core
    order = stat_own.shape[0]
    half = order // 2
    pieces = layout(half)
    chunks = len(pieces)
    parts = [(0, half // 2), (half // 2, half // 2), (half, half)]
    height = grad_own.shape[1]

    def at(offset):
        return lax.rem(me + sign * offset + 4 * ring, ring)

    def to(offset):
        return {"mp": at(offset)}

    stat_copy = pltpu.make_async_copy(stat_ref.at[0], stat_own, local_sem.at[0])
    grad_copy = pltpu.make_async_copy(grad_ref.at[0], grad_own, local_sem.at[1])
    grad_copy.start()
    stat_copy.start()

    barrier = pltpu.get_barrier_semaphore()
    pl.semaphore_signal(barrier, inc=1, device_id=sibling, device_id_type=MESH)
    span = max(1, ring // 2 - reach)
    direct = 1 if RELAY else span
    for d in range(1, direct + 1):
        pl.semaphore_signal(barrier, inc=1, device_id=to(d), device_id_type=MESH)
        pl.semaphore_signal(barrier, inc=1, device_id=to(-d), device_id_type=MESH)
    pl.semaphore_wait(barrier, 2 * direct + 1)

    def tell(d):
        if RELAY and d <= span:
            pl.semaphore_signal(ready.at[0, d], inc=1, device_id=to(1), device_id_type=MESH)
            pl.semaphore_signal(ready.at[1, d], inc=1, device_id=to(-1), device_id_type=MESH)

    def heard(d):
        if RELAY and 1 < d <= span:
            pl.semaphore_wait(ready.at[0, d], 1)
            pl.semaphore_wait(ready.at[1, d], 1)
            tell(d + 1)

    tell(2)

    def grad_swap(block, near=False):
        j = 0 if near else lax.rem(block - me + ring, ring)
        return pltpu.make_async_remote_copy(
            src_ref=grad_ref.at[1, block],
            dst_ref=grad_sib.at[block],
            send_sem=sib_send.at[0],
            recv_sem=sib_recv.at[j],
            device_id=sibling,
            device_id_type=MESH,
        )

    stat_swap = pltpu.make_async_remote_copy(
        src_ref=stat_ref.at[1],
        dst_ref=stat_sib,
        send_sem=sib_send.at[1],
        recv_sem=sib_recv.at[1],
        device_id=sibling,
        device_id_type=MESH,
    )
    far_sides = [(1, ring // 2 - reach)]
    for k in range(ring // 2 - reach - 1, 0, -1):
        far_sides += [(1, k), (0, k)]
    nearest_first = far_sides[::-1]
    row_order = nearest_first if RELAY else far_sides

    def far_block(side, k):
        return at((1 if side else -1) * (reach + k))

    for side, k in row_order:
        grad_swap(far_block(side, k)).start()
    stat_swap.start()
    for d in range(-reach, reach + 1):
        grad_swap(at(d), near=True).start()

    own_first = counts_ref[0] >= 1

    def select_rows(block):
        grad_sel[block] = jnp.where(own_first, grad_own[block], grad_sib[block])

    def row_copy(side, k):
        way = 1 if side else -1
        return pltpu.make_async_remote_copy(
            src_ref=grad_sel.at[far_block(side, k)],
            dst_ref=request.at[side, pl.ds(k * height, height)],
            send_sem=row_send.at[0],
            recv_sem=row_recv.at[0],
            device_id=to(way * k),
            device_id_type=MESH,
        )

    grad_copy.wait()
    heard(2)
    last = 2
    for side, k in row_order:
        grad_swap(far_block(side, k)).wait_recv()
        select_rows(far_block(side, k))
        while last < k:
            last += 1
            heard(last)
        row_copy(side, k).start()

    stat_copy.wait()
    stat_swap.wait_recv()
    pack(newton_root(jnp.where(own_first, stat_own[...], stat_sib[...])), own_root)

    def piece(c):
        return pl.ds(*pieces[c])

    def root_copy(side, d, c):
        source = own_root if d == 1 else roots.at[side, d - 2]
        return pltpu.make_async_remote_copy(
            src_ref=source.at[piece(c)],
            dst_ref=roots.at[side, d - 1, piece(c)],
            send_sem=root_send.at[0],
            recv_sem=root_recv.at[side, d - 1, c],
            device_id=to(-1 if side else 1),
            device_id_type=MESH,
        )

    for c in range(chunks):
        for side in range(2):
            root_copy(side, 1, c).start()

    def all_here(place, sem):
        pltpu.make_async_remote_copy(
            src_ref=place,
            dst_ref=place,
            send_sem=sib_send.at[0],
            recv_sem=sem,
            device_id=sibling,
            device_id_type=MESH,
        ).wait_recv()

    all_here(grad_sib.at[pl.ds(0, 2 * reach + 1)], sib_recv.at[0])
    for d in range(-reach, reach + 1):
        select_rows(at(d))

    def out_copies(source, own, other):
        local = pltpu.make_async_copy(source, own, out_sem.at[0])
        remote = pltpu.make_async_remote_copy(
            src_ref=source,
            dst_ref=other,
            send_sem=out_sem.at[1],
            recv_sem=out_sem.at[2],
            device_id=sibling,
            device_id_type=MESH,
        )
        return local, remote

    def send_out(offset, start=0, width=order):
        place = (at(offset), slice(None), pl.ds(start, width))
        for copy in out_copies(result.at[place], out_ref.at[(0, *place)], out_ref.at[(1, *place)]):
            copy.start()

    result[me] = apply_root(grad_sel[me], own_root)
    send_out(0)

    for d in range(1, reach):
        for c in range(chunks):
            for side in range(2):
                root_copy(side, d, c).wait_recv()
                root_copy(side, d + 1, c).start()
        for side in range(2):
            offset = d if side else -d
            result[at(offset)] = apply_root(grad_sel[at(offset)], roots.at[side, d - 1])
            send_out(offset)

    def back_copy(side, k, part):
        way = 1 if side else -1
        return pltpu.make_async_remote_copy(
            src_ref=answer.at[side, pl.ds(k * height, height), pl.ds(*parts[part])],
            dst_ref=result.at[at(way * reach), :, pl.ds(*parts[part])],
            send_sem=back_send.at[0],
            recv_sem=back_recv.at[side, k if part == 2 else 0],
            device_id=to(-way * k),
            device_id_type=MESH,
        )

    def arrived(side, k, part):
        way = 1 if side else -1
        return pltpu.make_async_remote_copy(
            src_ref=answer.at[side, pl.ds(k * height, height), pl.ds(*parts[part])],
            dst_ref=result.at[at(way * (reach + k)), :, pl.ds(*parts[part])],
            send_sem=back_send.at[0],
            recv_sem=back_recv.at[side, k if part == 2 else 0],
            device_id=to(way * k),
            device_id_type=MESH,
        )

    served = [[k for s, k in far_sides if s == side] for side in range(2)]
    all_here(grad_sel.at[pl.ds(0, len(far_sides))], row_recv.at[0])
    for part, needed in ((0, (0, 1)), (1, (2,)), (2, (3,))):
        for side in (1, 0):
            rows = slice(height, (len(served[side]) + 1) * height)
            start, width = parts[part]
            for c in needed:
                root_copy(side, reach, c).wait_recv()
            answer[side, rows, start : start + width] = apply_part(
                request[side, rows], roots.at[side, reach - 1], part
            )
            for k in served[side]:
                back_copy(side, k, part).start()
    for side in (1, 0):
        offset = reach if side else -reach
        result[at(offset)] = apply_root(grad_sel[at(offset)], roots.at[side, reach - 1])
        send_out(offset)

    def all_sent(source, sem):
        pltpu.make_async_remote_copy(
            src_ref=source,
            dst_ref=source,
            send_sem=sem,
            recv_sem=sib_recv.at[0],
            device_id=sibling,
            device_id_type=MESH,
        ).wait_send()

    all_sent(grad_sib, sib_send.at[0])
    all_sent(stat_sib, sib_send.at[1])
    all_sent(grad_sel.at[pl.ds(0, len(far_sides))], row_send.at[0])
    all_sent(roots, root_send.at[0])

    for side in range(2):
        all_here(answer.at[side, pl.ds(0, len(served[side]) * height), pl.ds(0, half)], back_recv.at[side, 0])
    for side, k in far_sides:
        send_out((1 if side else -1) * (reach + k), 0, half)
    for side, k in far_sides:
        arrived(side, k, 2).wait_recv()
        send_out((1 if side else -1) * (reach + k), half, half)
    all_sent(grad_sel.at[pl.ds(0, len(far_sides))], back_send.at[0])
    for copy in out_copies(result, out_ref.at[0], out_ref.at[1]):
        copy.wait()


def keep_live(counts_ref, in_ref, out_ref, zeros, sem):
    zeros[...] = jnp.zeros_like(zeros)
    slots, blocks = in_ref.shape[:2]
    depth = blocks // CUTS

    def copy(slot, cut, live):
        place = (slot, pl.ds(cut * depth, depth))
        source = in_ref.at[place] if live else zeros
        return pltpu.make_async_copy(source, out_ref.at[place], sem.at[slot, cut])

    for slot in range(slots):

        @pl.when(counts_ref[0] > slot)
        def _():
            for cut in range(CUTS):
                copy(slot, cut, True).start()

        @pl.when(counts_ref[0] <= slot)
        def _():
            for cut in range(CUTS):
                copy(slot, cut, False).start()

    for slot in range(slots):
        for cut in range(CUTS):
            copy(slot, cut, True).wait()


def on_device(mesh, statistics, gradients, counts):
    ring = mesh.shape["mp"]
    reach = REACH
    slots, blocks, height, order = gradients.shape
    half = order // 2
    pieces = layout(half)
    chunks, packed = len(pieces), sum(pieces[-1])
    tall = (ring // 2 - reach + 1) * height
    anywhere = pl.BlockSpec(memory_space=pl.ANY)
    in_hbm = pl.BlockSpec(memory_space=pltpu.HBM)
    dma = pltpu.SemaphoreType.DMA
    out = pl.pallas_call(
        functools.partial(kernel, ring, reach),
        out_shape=jax.ShapeDtypeStruct(gradients.shape, BF16),
        in_specs=[pl.BlockSpec(memory_space=pltpu.SMEM), in_hbm, in_hbm],
        out_specs=anywhere,
        scratch_shapes=[
            pltpu.VMEM((order, order), BF16),
            pltpu.VMEM((order, order), BF16),
            pltpu.VMEM((blocks, height, order), BF16),
            pltpu.VMEM((blocks, height, order), BF16),
            pltpu.VMEM((blocks, height, order), BF16),
            pltpu.VMEM((2, tall, order), BF16),
            pltpu.VMEM((2, tall, order), BF16),
            pltpu.VMEM((packed, LANES), BF16),
            pltpu.VMEM((2, reach, packed, LANES), BF16),
            pltpu.VMEM((blocks, height, order), BF16),
            dma((2,)),
            dma((2,)),
            dma((ring - reach,)),
            dma((1,)),
            dma((1,)),
            dma((1,)),
            dma((2, reach, chunks)),
            dma((1,)),
            dma((2, ring // 2 - reach + 1)),
            dma((3,)),
            pltpu.SemaphoreType.REGULAR((2, ring // 2 - reach + 1)),
        ],
        compiler_params=pltpu.CompilerParams(
            collective_id=0, has_side_effects=True, vmem_limit_bytes=52 * 1024 * 1024
        ),
        name="hybrid",
    )(counts, statistics, gradients)
    return pl.pallas_call(
        keep_live,
        out_shape=jax.ShapeDtypeStruct(gradients.shape, BF16),
        in_specs=[pl.BlockSpec(memory_space=pltpu.SMEM), anywhere],
        out_specs=anywhere,
        scratch_shapes=[pltpu.VMEM((blocks // CUTS, height, order), BF16), dma((slots, CUTS))],
        compiler_params=pltpu.CompilerParams(vmem_limit_bytes=8 * 1024 * 1024),
        name="keep_live",
    )(counts, out)


def solution(mesh):
    in_specs = (P("dp", "mp", None), P("dp", None, "mp", None), P("dp"))
    out_specs = P("dp", None, "mp", None)
    return jax.shard_map(
        functools.partial(on_device, mesh),
        mesh=mesh,
        in_specs=in_specs,
        out_specs=out_specs,
        check_vma=False,
    )
```

```python
import functools

import jax
import jax.numpy as jnp
from jax import lax
from jax.experimental import pallas as pl
from jax.experimental.pallas import tpu as pltpu
from jax.sharding import PartitionSpec as P

MESH = pl.DeviceIdType.MESH
LANES = 128
TAIL = 16
REACH = 4
RELAY = True
F32 = jnp.float32
BF16 = jnp.bfloat16


def dot(a, b):
    return jnp.dot(a, b, preferred_element_type=F32)


def dot_t(a, b):
    return lax.dot_general(a, b, (((1,), (1,)), ((), ())), preferred_element_type=F32)


def iotas(shape):
    return lax.broadcasted_iota(jnp.int32, shape, 0), lax.broadcasted_iota(jnp.int32, shape, 1)


def newton_root(block):
    order = block.shape[0]
    values = block.astype(F32)
    total = jnp.sum(jnp.sum(values * values, axis=1, keepdims=True), axis=0, keepdims=True)
    norm_scale = jnp.sqrt(total) + 1e-06
    scaled = (values * (1.0 / norm_scale)).astype(BF16)
    row, column = iotas((order, order))
    five = jnp.where(row == column, 5.0, 0.0).astype(F32)
    step_one = ((five - scaled.astype(F32)) * 0.25).astype(BF16)
    square = dot(step_one, step_one).astype(BF16)
    fourth = dot(square, square).astype(BF16)
    updated = dot(fourth, scaled)
    step_two = ((five - updated) * 0.25).astype(BF16)
    return dot(step_one, step_two) * lax.rsqrt(jnp.sqrt(norm_scale))


def layout(half):
    size = half * half // 2 // LANES
    lengths = [size, size + TAIL, size, size]
    return [(sum(lengths[:n]), lengths[n]) for n in range(len(lengths))]


def fold(block):
    size = block.shape[0] // 2
    row, column = iotas((size, size))
    corner = block[size:, size:]
    both = jnp.where(row <= column, block[:size, :size], corner)
    diagonal = jnp.sum(jnp.where(row == column, corner, 0.0), axis=0, keepdims=True)
    return block[:size, size:].astype(BF16), both.astype(BF16), diagonal


def unfold(above, both, diagonal):
    size = both.shape[0]
    row, column = iotas((size, size))
    both = both.astype(F32)
    mirror = both.T
    first = jnp.where(row <= column, both, mirror).astype(BF16)
    last = jnp.where(row > column, both, jnp.where(row == column, diagonal, mirror)).astype(BF16)
    below = above.astype(F32).T.astype(BF16)
    return jnp.concatenate(
        [jnp.concatenate([first, above], axis=1), jnp.concatenate([below, last], axis=1)], axis=0
    )


def store_slabs(ref, start, block):
    height, width = block.shape
    for j in range(width // LANES):
        ref[start + j * height : start + (j + 1) * height, :] = block[:, j * LANES : (j + 1) * LANES]
    return start + height * width // LANES


def load_slabs(ref, start, height, width):
    slabs = [ref[start + j * height : start + (j + 1) * height, :] for j in range(width // LANES)]
    return jnp.concatenate(slabs, axis=1) if len(slabs) > 1 else slabs[0]


def pack(root, ref):
    half = root.shape[0] // 2
    size = half // 2
    starts = [start for start, _ in layout(half)]
    across = root[:half, half:].astype(BF16)
    above_0, both_0, diagonal_0 = fold(root[:half, :half])
    above_1, both_1, diagonal_1 = fold(root[half:, half:])
    store_slabs(ref, starts[0], across[:size])
    end = store_slabs(ref, store_slabs(ref, starts[1], above_0), both_0)
    tail_row, _ = iotas((TAIL, size))
    tail = jnp.where(tail_row == 0, diagonal_0, jnp.where(tail_row == 1, diagonal_1, 0.0))
    ref[end : end + TAIL, :] = tail.astype(BF16)
    store_slabs(ref, starts[2], across[size:])
    store_slabs(ref, store_slabs(ref, starts[3], above_1), both_1)


def unpack_across(ref, half, which):
    return load_slabs(ref, layout(half)[2 * which][0], half // 2, half)


def unpack_corner(ref, half, which):
    size = half // 2
    starts = [start for start, _ in layout(half)]
    start = starts[1 + 2 * which]
    above = load_slabs(ref, start, size, size)
    both = load_slabs(ref, start + size * size // LANES, size, size)
    tail = ref[starts[2] - TAIL : starts[2], :].astype(F32)
    return unfold(above, both, tail[which : which + 1, :])


def apply_part(rows, ref, part):
    half = rows.shape[1] // 2
    size = half // 2
    left, right = rows[:, :half], rows[:, half:]
    if part < 2:
        corner = unpack_corner(ref, half, 0)[:, part * size : (part + 1) * size]
        return (dot(left, corner) + dot_t(right, unpack_across(ref, half, part))).astype(BF16)
    across = jnp.concatenate([unpack_across(ref, half, 0), unpack_across(ref, half, 1)], axis=0)
    return (dot(left, across) + dot(right, unpack_corner(ref, half, 1))).astype(BF16)


def apply_root(rows, ref):
    half = rows.shape[1] // 2
    left, right = rows[:, :half], rows[:, half:]
    across = jnp.concatenate([unpack_across(ref, half, 0), unpack_across(ref, half, 1)], axis=0)
    out_left = dot(left, unpack_corner(ref, half, 0)) + dot_t(right, across)
    out_right = dot(left, across) + dot(right, unpack_corner(ref, half, 1))
    return jnp.concatenate([out_left, out_right], axis=1).astype(BF16)


def kernel(
    ring,
    reach,
    counts_ref,
    stat_ref,
    grad_ref,
    out_ref,
    stat_own,
    stat_sib,
    grad_own,
    grad_sib,
    grad_sel,
    request,
    answer,
    own_root,
    roots,
    result,
    local_sem,
    sib_send,
    sib_recv,
    row_send,
    row_recv,
    root_send,
    root_recv,
    back_send,
    back_recv,
    out_sem,
    ready,
):
    dp, me = lax.axis_index("dp"), lax.axis_index("mp")
    core = lax.rem(dp, 2)
    sibling = {"dp": dp + 1 - 2 * core}
    sign = 1 - 2 * core
    order = stat_own.shape[0]
    half = order // 2
    pieces = layout(half)
    chunks = len(pieces)
    parts = [(0, half // 2), (half // 2, half // 2), (half, half)]
    height = grad_own.shape[1]

    def at(offset):
        return lax.rem(me + sign * offset + 4 * ring, ring)

    def to(offset):
        return {"mp": at(offset)}

    stat_copy = pltpu.make_async_copy(stat_ref.at[0], stat_own, local_sem.at[0])
    grad_copy = pltpu.make_async_copy(grad_ref.at[0], grad_own, local_sem.at[1])
    grad_copy.start()
    stat_copy.start()

    barrier = pltpu.get_barrier_semaphore()
    pl.semaphore_signal(barrier, inc=1, device_id=sibling, device_id_type=MESH)
    span = max(1, ring // 2 - reach)
    direct = 1 if RELAY else span
    for d in range(1, direct + 1):
        pl.semaphore_signal(barrier, inc=1, device_id=to(d), device_id_type=MESH)
        pl.semaphore_signal(barrier, inc=1, device_id=to(-d), device_id_type=MESH)
    pl.semaphore_wait(barrier, 2 * direct + 1)

    def tell(d):
        if RELAY and d <= span:
            pl.semaphore_signal(ready.at[0, d], inc=1, device_id=to(1), device_id_type=MESH)
            pl.semaphore_signal(ready.at[1, d], inc=1, device_id=to(-1), device_id_type=MESH)

    def heard(d):
        if RELAY and 1 < d <= span:
            pl.semaphore_wait(ready.at[0, d], 1)
            pl.semaphore_wait(ready.at[1, d], 1)
            tell(d + 1)

    tell(2)

    def grad_swap(block, near=False):
        j = 0 if near else lax.rem(block - me + ring, ring)
        return pltpu.make_async_remote_copy(
            src_ref=grad_ref.at[1, block],
            dst_ref=grad_sib.at[block],
            send_sem=sib_send.at[0],
            recv_sem=sib_recv.at[j],
            device_id=sibling,
            device_id_type=MESH,
        )

    stat_swap = pltpu.make_async_remote_copy(
        src_ref=stat_ref.at[1],
        dst_ref=stat_sib,
        send_sem=sib_send.at[1],
        recv_sem=sib_recv.at[1],
        device_id=sibling,
        device_id_type=MESH,
    )
    far_sides = [(1, ring // 2 - reach)]
    for k in range(ring // 2 - reach - 1, 0, -1):
        far_sides += [(1, k), (0, k)]
    nearest_first = far_sides[::-1]
    row_order = nearest_first if RELAY else far_sides

    def far_block(side, k):
        return at((1 if side else -1) * (reach + k))

    for side, k in row_order:
        grad_swap(far_block(side, k)).start()
    stat_swap.start()
    for d in range(-reach, reach + 1):
        grad_swap(at(d), near=True).start()

    own_first = counts_ref[0] >= 1

    def select_rows(block):
        grad_sel[block] = jnp.where(own_first, grad_own[block], grad_sib[block])

    def row_copy(side, k):
        way = 1 if side else -1
        return pltpu.make_async_remote_copy(
            src_ref=grad_sel.at[far_block(side, k)],
            dst_ref=request.at[side, pl.ds(k * height, height)],
            send_sem=row_send.at[0],
            recv_sem=row_recv.at[0],
            device_id=to(way * k),
            device_id_type=MESH,
        )

    grad_copy.wait()
    heard(2)
    last = 2
    for side, k in row_order:
        grad_swap(far_block(side, k)).wait_recv()
        select_rows(far_block(side, k))
        while last < k:
            last += 1
            heard(last)
        row_copy(side, k).start()

    stat_copy.wait()
    stat_swap.wait_recv()
    pack(newton_root(jnp.where(own_first, stat_own[...], stat_sib[...])), own_root)

    def piece(c):
        return pl.ds(*pieces[c])

    def root_copy(side, d, c):
        source = own_root if d == 1 else roots.at[side, d - 2]
        return pltpu.make_async_remote_copy(
            src_ref=source.at[piece(c)],
            dst_ref=roots.at[side, d - 1, piece(c)],
            send_sem=root_send.at[0],
            recv_sem=root_recv.at[side, d - 1, c],
            device_id=to(-1 if side else 1),
            device_id_type=MESH,
        )

    for c in range(chunks):
        for side in range(2):
            root_copy(side, 1, c).start()

    def all_here(place, sem):
        pltpu.make_async_remote_copy(
            src_ref=place,
            dst_ref=place,
            send_sem=sib_send.at[0],
            recv_sem=sem,
            device_id=sibling,
            device_id_type=MESH,
        ).wait_recv()

    all_here(grad_sib.at[pl.ds(0, 2 * reach + 1)], sib_recv.at[0])
    for d in range(-reach, reach + 1):
        select_rows(at(d))

    def out_copies(source, own, other):
        local = pltpu.make_async_copy(source, own, out_sem.at[0])
        remote = pltpu.make_async_remote_copy(
            src_ref=source,
            dst_ref=other,
            send_sem=out_sem.at[1],
            recv_sem=out_sem.at[2],
            device_id=sibling,
            device_id_type=MESH,
        )
        return local, remote

    def send_out(offset, start=0, width=order):
        place = (at(offset), slice(None), pl.ds(start, width))
        for copy in out_copies(result.at[place], out_ref.at[(0, *place)], out_ref.at[(1, *place)]):
            copy.start()

    result[me] = apply_root(grad_sel[me], own_root)
    send_out(0)

    def use_here(side, d):
        offset = d if side else -d
        result[at(offset)] = apply_root(grad_sel[at(offset)], roots.at[side, d - 1])
        send_out(offset)

    for d in range(1, reach):
        for c in range(chunks):
            for side in range(2):
                root_copy(side, d, c).wait_recv()
                root_copy(side, d + 1, c).start()
            if d > 1 and c < 2:
                use_here(c, d - 1)

    def back_copy(side, k, part):
        way = 1 if side else -1
        return pltpu.make_async_remote_copy(
            src_ref=answer.at[side, pl.ds(k * height, height), pl.ds(*parts[part])],
            dst_ref=result.at[at(way * reach), :, pl.ds(*parts[part])],
            send_sem=back_send.at[0],
            recv_sem=back_recv.at[side, k if part == 2 else 0],
            device_id=to(-way * k),
            device_id_type=MESH,
        )

    def arrived(side, k, part):
        way = 1 if side else -1
        return pltpu.make_async_remote_copy(
            src_ref=answer.at[side, pl.ds(k * height, height), pl.ds(*parts[part])],
            dst_ref=result.at[at(way * (reach + k)), :, pl.ds(*parts[part])],
            send_sem=back_send.at[0],
            recv_sem=back_recv.at[side, k if part == 2 else 0],
            device_id=to(way * k),
            device_id_type=MESH,
        )

    served = [[k for s, k in far_sides if s == side] for side in range(2)]
    all_here(grad_sel.at[pl.ds(0, len(far_sides))], row_recv.at[0])
    for part, needed in ((0, (0, 1)), (1, (2,)), (2, (3,))):
        for side in (1, 0):
            rows = slice(height, (len(served[side]) + 1) * height)
            start, width = parts[part]
            for c in needed:
                root_copy(side, reach, c).wait_recv()
            answer[side, rows, start : start + width] = apply_part(
                request[side, rows], roots.at[side, reach - 1], part
            )
            for k in served[side]:
                back_copy(side, k, part).start()
    for side in range(2):
        use_here(side, reach - 1)
    for side in (1, 0):
        offset = reach if side else -reach
        result[at(offset)] = apply_root(grad_sel[at(offset)], roots.at[side, reach - 1])
        send_out(offset)

    def all_sent(source, sem):
        pltpu.make_async_remote_copy(
            src_ref=source,
            dst_ref=source,
            send_sem=sem,
            recv_sem=sib_recv.at[0],
            device_id=sibling,
            device_id_type=MESH,
        ).wait_send()

    all_sent(grad_sib, sib_send.at[0])
    all_sent(stat_sib, sib_send.at[1])
    all_sent(grad_sel.at[pl.ds(0, len(far_sides))], row_send.at[0])
    all_sent(roots, root_send.at[0])

    for side in range(2):
        all_here(answer.at[side, pl.ds(0, len(served[side]) * height), pl.ds(0, half)], back_recv.at[side, 0])
    for side, k in far_sides:
        send_out((1 if side else -1) * (reach + k), 0, half)
    for side, k in far_sides:
        arrived(side, k, 2).wait_recv()
        send_out((1 if side else -1) * (reach + k), half, half)
    all_sent(grad_sel.at[pl.ds(0, len(far_sides))], back_send.at[0])
    for copy in out_copies(result, out_ref.at[0], out_ref.at[1]):
        copy.wait()


def on_device(mesh, statistics, gradients, counts):
    ring = mesh.shape["mp"]
    reach = REACH
    slots, blocks, height, order = gradients.shape
    half = order // 2
    pieces = layout(half)
    chunks, packed = len(pieces), sum(pieces[-1])
    tall = (ring // 2 - reach + 1) * height
    anywhere = pl.BlockSpec(memory_space=pl.ANY)
    in_hbm = pl.BlockSpec(memory_space=pltpu.HBM)
    dma = pltpu.SemaphoreType.DMA
    out = pl.pallas_call(
        functools.partial(kernel, ring, reach),
        out_shape=jax.ShapeDtypeStruct(gradients.shape, BF16),
        in_specs=[pl.BlockSpec(memory_space=pltpu.SMEM), in_hbm, in_hbm],
        out_specs=anywhere,
        scratch_shapes=[
            pltpu.VMEM((order, order), BF16),
            pltpu.VMEM((order, order), BF16),
            pltpu.VMEM((blocks, height, order), BF16),
            pltpu.VMEM((blocks, height, order), BF16),
            pltpu.VMEM((blocks, height, order), BF16),
            pltpu.VMEM((2, tall, order), BF16),
            pltpu.VMEM((2, tall, order), BF16),
            pltpu.VMEM((packed, LANES), BF16),
            pltpu.VMEM((2, reach, packed, LANES), BF16),
            pltpu.VMEM((blocks, height, order), BF16),
            dma((2,)),
            dma((2,)),
            dma((ring - reach,)),
            dma((1,)),
            dma((1,)),
            dma((1,)),
            dma((2, reach, chunks)),
            dma((1,)),
            dma((2, ring // 2 - reach + 1)),
            dma((3,)),
            pltpu.SemaphoreType.REGULAR((2, ring // 2 - reach + 1)),
        ],
        compiler_params=pltpu.CompilerParams(
            collective_id=0, has_side_effects=True, vmem_limit_bytes=52 * 1024 * 1024
        ),
        name="hybrid",
    )(counts, statistics, gradients)
    live = (jnp.arange(slots) < counts[0])[:, None, None, None]
    return jnp.where(live, out, jnp.zeros_like(out))


def solution(mesh):
    in_specs = (P("dp", "mp", None), P("dp", None, "mp", None), P("dp"))
    out_specs = P("dp", None, "mp", None)
    return jax.shard_map(
        functools.partial(on_device, mesh),
        mesh=mesh,
        in_specs=in_specs,
        out_specs=out_specs,
        check_vma=False,
    )
```
